256 devices in a mesh: seq: 64 (over y, z, core), mp: 4 (over x).
Axes of the slice: x: 4, y: 4, z: 8, core: 2. Of those that a mesh axis runs over, the one named last changes fastest.
Arguments:
- phoneme_rows: bfloat16 [8192, 1024], P('seq'), may hold values from -6 to 6
- durations: int32 [8192], P('seq'), may hold values from 1 to 40, as said below
- conv_first: bfloat16 [3, 1024, 512], P(None, None, 'mp'), may hold values from -0.109375 to 0.109375
- conv_second: bfloat16 [2, 3, 256, 256], replicated, may hold values from -0.21875 to 0.21875
- readout: bfloat16 [2, 256], replicated, may hold values from -0.375 to 0.375
- targets: float32 [2, 65536], P(None, 'seq'), may hold values from -6 to 6
Outputs:
- predicted: float32 [2, 65536], P(None, 'seq')
- row_grad: bfloat16 [8192, 1024], P('seq', 'mp')
The draws below stay inside these ranges and needn't reach their ends.
Inputs may be any that keep to these rules, and one draw needn't show every extreme that they name: The durations sum to 65536. In every aligned block of 128 phonemes one phoneme lasts 40 frames and another 1 frame. Every frame from d * 1024 - 2 to (d + 1) * 1024 + 1 that lies in the window belongs to a phoneme of seq indices d - 2 to d + 2, and in every draw some frames need phonemes 2 indices away.
All inputs are finite; a program needn't handle non-finite values.
Results may differ from the reference program's by a relative error of at most 0.015.
Values may be sent and summed in bfloat16 or wider, within the bound.
No kernel may reach another device: no remote copies, remote signals or barrier semaphores. Data moves between devices by JAX's collectives and lax.ppermute only.
A program may use at most 64 MiB of HBM per device.

```python
import jax
import jax.numpy as jnp
from jax import lax

D = 1024
C = 256
PH_DEV = 128
PHONEMES = 8192
FRAMES = 65536


def draw_durations(key, part):
    key = jax.random.fold_in(key, 7)
    blocks = PHONEMES // PH_DEV
    groups = blocks // 4
    subkeys = jax.random.split(key, 5)
    strong = jax.random.randint(subkeys[0], (groups,), 17 * PH_DEV // 4, 9 * PH_DEV // 2 + 1)
    directions = 2 * jax.random.randint(subkeys[1], (groups,), 0, 2) - 1
    gentle = jax.random.randint(subkeys[2], (groups - 1,), -(3 * PH_DEV // 2), 3 * PH_DEV // 2 + 1)
    pattern = jnp.array([1, 1, -1, -1], dtype=jnp.int32)
    broad_steps = ((strong * directions)[:, None] * pattern[None, :]).reshape(-1)
    narrow = (gentle[:, None] * pattern[None, :]).reshape(-1)
    narrow = jnp.concatenate([jnp.zeros((2,), jnp.int32), narrow, jnp.zeros((2,), jnp.int32)])
    totals = 8 * PH_DEV + broad_steps + narrow
    ordering_lookup = jax.vmap(lambda subkey: jax.random.permutation(subkey, PH_DEV))(jax.random.split(subkeys[3], blocks))
    weights = jax.random.randint(subkeys[4], (blocks, PH_DEV), 2, 5)
    weights = jnp.where(ordering_lookup >= 2, weights, 0)
    spare_frames = totals - PH_DEV - 39
    baseline_surplus = spare_frames[:, None] * weights // jnp.sum(weights, axis=1, keepdims=True)
    remainder_frames = spare_frames - jnp.sum(baseline_surplus, axis=1)
    additional_frame = ((ordering_lookup >= 2) & (ordering_lookup < 2 + remainder_frames[:, None])).astype(jnp.int32)
    surplus_frames = jnp.where(ordering_lookup == 0, 39, baseline_surplus + additional_frame)
    return (1 + surplus_frames).reshape(-1).astype(jnp.int32)


def level_of(stream_key, extent, shards, least, top_value):
    gain = 1.0
    for dim, shards_of in shards:
        heights = jax.random.uniform(jax.random.fold_in(jax.random.fold_in(stream_key, 6), dim), (shards_of,), jnp.float32, least / len(shards), top_value / len(shards))
        gain = gain * jnp.repeat(jnp.exp(heights), extent[dim] // shards_of).reshape((-1,) + (1,) * (len(extent) - 1 - dim))
    return gain


def normal_values(rng, shape, scale, limit, cuts=(), held_as=jnp.bfloat16):
    drawn = scale * jax.random.normal(rng, shape, jnp.float32)
    if cuts:
        drawn = drawn * level_of(rng, shape, cuts, -0.22, 0.18)
    return jnp.clip(drawn, -limit, limit).astype(held_as)


def setup_inputs(seed: int = 0) -> dict:
    splits = jax.random.split(jax.random.key(seed), 7)
    return {
        "phoneme_rows": normal_values(splits[0], (PHONEMES, D), 1.0, 6.0, ((0, 64),)),
        "durations": draw_durations(jax.random.fold_in(splits[6], 71), 0),
        "conv_first": normal_values(splits[2], (3, D, 2 * C), (3 * D) ** -0.5, 0.109375, ((2, 4),)),
        "conv_second": normal_values(splits[3], (2, 3, C, C), (3 * C) ** -0.5, 0.21875),
        "readout": normal_values(splits[4], (2, C), C ** -0.5, 0.375),
        "targets": normal_values(splits[5], (2, FRAMES), 1.0, 6.0, ((1, 64),), jnp.float32),
    }


epsilon = 1e-05

def layer_standardize(values):
    average = lax.optimization_barrier(jnp.mean(values, axis=-1, keepdims=True))
    centered = values - average
    variance = lax.optimization_barrier(jnp.mean(centered * centered, axis=-1, keepdims=True))
    inverse = lax.rsqrt(variance + epsilon)
    return (centered * inverse, inverse)

def normalize_back(gradient, normed, inverse):
    first_mean = lax.optimization_barrier(jnp.mean(gradient, axis=-1, keepdims=True))
    second_mean = lax.optimization_barrier(jnp.mean(gradient * normed, axis=-1, keepdims=True))
    return inverse * (gradient - first_mean - normed * second_mean)

def conv_same(inputs, kernel):
    length = inputs.shape[0]
    padded = jnp.pad(inputs, ((1, 1), (0, 0)))
    summed = jnp.dot(padded[0:length], kernel[0], preferred_element_type=jnp.float32)
    for kernel_index in range(1, 3):
        summed = summed + jnp.dot(padded[kernel_index:kernel_index + length], kernel[kernel_index], preferred_element_type=jnp.float32)
    return summed

def conv_back(gradient, kernel):
    length = gradient.shape[0]
    padded = jnp.pad(gradient, ((1, 1), (0, 0)))
    summed = jnp.zeros((length, kernel.shape[1]), jnp.float32)
    for kernel_index in range(3):
        low_edge = 2 - kernel_index
        summed = summed + jnp.dot(padded[low_edge:low_edge + length], kernel[kernel_index].T, preferred_element_type=jnp.float32)
    return summed

def reference(phoneme_rows, durations, conv_first, conv_second, readout, targets):
    owners = jnp.repeat(jnp.arange(PHONEMES, dtype=jnp.int32), durations, total_repeat_length=FRAMES)
    frames = jnp.take(phoneme_rows, owners, axis=0)
    first_conv = conv_same(frames, conv_first)
    first_act = jax.nn.softplus(first_conv).astype(jnp.bfloat16)
    act_split = first_act.astype(jnp.float32).reshape(FRAMES, 2, C)
    normed_one, inverse_one = layer_standardize(act_split)
    hidden = normed_one.astype(jnp.bfloat16)
    second = jnp.stack([conv_same(hidden[:, predictor], conv_second[predictor]) for predictor in range(2)], axis=1)
    standardized_second, inverse_two = layer_standardize(jax.nn.softplus(second))
    weights = readout.astype(jnp.float32)
    predicted = lax.optimization_barrier(jnp.sum(standardized_second * weights, axis=-1))
    residual = predicted - targets.T
    grad_second = (normalize_back(residual[:, :, None] * weights, standardized_second, inverse_two) * jax.nn.sigmoid(second)).astype(jnp.bfloat16)
    grad_hidden = jnp.stack([conv_back(grad_second[:, predictor], conv_second[predictor]) for predictor in range(2)], axis=1)
    grad_first = (normalize_back(grad_hidden, normed_one, inverse_one) * (1.0 - jnp.exp(-act_split))).astype(jnp.bfloat16)
    grad_frames = conv_back(grad_first.reshape(FRAMES, 2 * C), conv_first)
    row_grad = jax.ops.segment_sum(grad_frames, owners, num_segments=PHONEMES)
    return (predicted.T, row_grad.astype(jnp.bfloat16))
```

```python
import functools

import jax
import jax.numpy as jnp
from jax import lax
from jax.experimental import pallas as pl
from jax.experimental.pallas import tpu as pltpu
from jax.sharding import PartitionSpec as P

EPSILON = 1e-05
TILE = 256
STRIDE = 252
LEAD = 3
HALO = 4
EDGE = 16
LONGEST = 40
REACH = 2
f32 = jnp.float32
bf16 = jnp.bfloat16
VMEM = pltpu.VMEM
SMEM = pltpu.SMEM


def whole():
    return pl.BlockSpec(memory_space=VMEM)


def copied(shape):
    return pl.BlockSpec(shape, lambda _: (0,) * len(shape))


def in_hbm(array):
    return pltpu.with_memory_space_constraint(array, pltpu.HBM)


def scalars():
    return pl.BlockSpec(memory_space=SMEM)


def call(kernel, name, *, flops=0, moved=0, vmem=24, **kwargs):
    return pl.pallas_call(
        kernel,
        name=name,
        grid=(1,),
        cost_estimate=pl.CostEstimate(flops=flops, bytes_accessed=moved, transcendentals=0),
        compiler_params=pltpu.CompilerParams(vmem_limit_bytes=vmem * 1024 * 1024),
        **kwargs,
    )


def rotate(block, axis, distance):
    size = lax.axis_size(axis)
    return lax.ppermute(block, axis, [(i, (i + distance) % size) for i in range(size)])


def pack_kernel(dur_ref, targets_ref, head_ref, tail_ref, to_right_ref, to_left_ref, spread_ref):
    block = dur_ref.shape[1]
    frames = targets_ref.shape[1]
    dur = dur_ref[...]
    rows = (tail_ref[...].astype(f32)[16 - HALO : 16], head_ref[...].astype(f32)[0:HALO])
    for out, halo in zip((to_right_ref, to_left_ref), rows):
        out[...] = jnp.zeros_like(out)
        out[0:2, 0:frames] = targets_ref[...]
        out[2:3, 0:block] = dur.astype(f32)
        out[HALO : 2 * HALO, :] = halo
    spread_ref[...] = jnp.broadcast_to(dur, spread_ref.shape)


def rows_kernel(where_ref, rows_ref, left_ref, right_ref, conv_ref, *refs):
    piece_refs, slice_refs, (table_ref,) = refs[:4], refs[4:8], refs[8:]
    taps, width, channels = conv_ref.shape
    members = len(piece_refs)
    block = rows_ref.shape[0]
    share = block // members
    features = width // members
    window = share + 2 * EDGE
    nothing = jnp.zeros((EDGE - HALO, width), f32)
    before = jnp.concatenate([nothing, left_ref[HALO : 2 * HALO]], axis=0).astype(bf16)
    after = jnp.concatenate([right_ref[HALO : 2 * HALO], nothing], axis=0).astype(bf16)
    rows = jnp.concatenate([before, rows_ref[...], after], axis=0)
    for k in range(taps):
        table_ref[k] = jnp.dot(rows, conv_ref[k], preferred_element_type=f32).astype(bf16)
    for d in range(members):
        target = lax.rem(where_ref[1] + d, members)
        at = pl.ds(pl.multiple_of(target * share, share), window)
        for k in range(taps):
            piece_refs[d][k * window : (k + 1) * window, :] = table_ref[k, at, :]
        slice_refs[d][...] = conv_ref[:, pl.ds(pl.multiple_of(target * features, features), features), :]


def share_bounds(where_ref, own_ref, left_ref, right_ref, last_seq, rows, first_row):
    block = 4 * (rows - 2 * (EDGE - first_row))
    share = block // 4
    s, m = where_ref[0], where_ref[1]
    lane = lax.broadcasted_iota(jnp.int32, (1, block), 1)
    near = jnp.where((lane >= block - HALO) & (s > 0), left_ref[2:3, 0:block], 0.0)
    far = jnp.where((lane < HALO) & (s < last_seq), right_ref[2:3, 0:block], 0.0)
    own = own_ref[2:3, 0:block]
    durations = jnp.concatenate([near, own, far], axis=1)
    phoneme = lax.broadcasted_iota(jnp.int32, (1, 3 * block), 1) - block
    begin = m * share
    row = lax.broadcasted_iota(jnp.int32, (rows, 3 * block), 0) + (begin + first_row - EDGE)
    at = jnp.broadcast_to(phoneme, (rows, 3 * block))
    spread = jnp.broadcast_to(durations, (rows, 3 * block))
    later = at >= begin

    def bound(limit):
        signed = jnp.where(later & (at < limit), spread, 0.0) - jnp.where(
            (at < begin) & (at >= limit), spread, 0.0
        )
        return jnp.sum(signed, axis=1, keepdims=True)

    count = jnp.sum(jnp.where((phoneme >= begin) & (phoneme < begin + share), durations, 0.0))
    skipped = jnp.sum(jnp.where((phoneme >= 0) & (phoneme < begin), durations, 0.0))
    return bound(row), bound(row + 1), count, skipped, jnp.sum(own)


def tiles_of(count):
    return lax.div(count.astype(jnp.int32) + (2 + STRIDE - 1), STRIDE)


def one_hot(frames, starts, ends):
    return jnp.where((frames >= starts) & (frames < ends), 1.0, 0.0).astype(bf16)


def local_frames(t):
    lane = lax.broadcasted_iota(jnp.int32, (1, TILE), 1)
    return (lane + (t * STRIDE - LEAD)).astype(f32), lane


def column_mean(values):
    return jnp.sum(values, axis=0, keepdims=True) * (1.0 / values.shape[0])


def with_neighbours(values):
    return jnp.concatenate(
        [
            pltpu.roll(values, 1, 1).astype(bf16),
            values.astype(bf16),
            pltpu.roll(values, TILE - 1, 1).astype(bf16),
        ],
        axis=0,
    )


def forward_kernel(
    last_seq,
    where_ref,
    own_ref,
    left_ref,
    right_ref,
    piece_ref,
    one_ref,
    two_ref,
    three_ref,
    conv_ref,
    readout_ref,
    pred_ref,
    far_ref,
    bounds_ref,
    table_ref,
    kernel_ref,
    weight_ref,
    kept_ref,
    sems,
):
    taps = conv_ref.shape[1]
    channels = conv_ref.shape[2]
    depth, chunk = piece_ref.shape
    window = depth // taps
    members = 2 * channels // chunk
    starts, ends, count, skipped, total = share_bounds(
        where_ref, own_ref, left_ref, right_ref, last_seq, window, 0
    )
    bounds_ref[0] = jnp.broadcast_to(starts, (window, TILE))
    bounds_ref[1] = jnp.broadcast_to(ends, (window, TILE))
    lowest = jnp.where(where_ref[0] == 0, -skipped, -1e9)
    end = jnp.where(where_ref[0] == last_seq, total - skipped, 1e9)
    for d, source in enumerate((piece_ref, one_ref, two_ref, three_ref)):
        owner = lax.rem(where_ref[1] + members - d, members)
        table_ref[pl.ds(pl.multiple_of(owner * chunk, chunk), chunk), :] = source[...].T
    for q in range(2):
        for k in range(taps):
            kernel_ref[q, :, k * channels : (k + 1) * channels] = conv_ref[q, k].T
        column = jnp.broadcast_to(readout_ref[q : q + 1, :].astype(f32), (8, channels)).T
        weight_ref[q] = jnp.broadcast_to(column[:, 0:1], (channels, TILE))

    def step(t, carry):
        frames, lane = local_frames(t)
        selector = jnp.concatenate(
            [one_hot(frames + (k - 1.0), bounds_ref[0], bounds_ref[1]) for k in range(taps)], axis=0
        )
        inside = jnp.where((frames >= lowest) & (frames < end), 1.0, 0.0)
        answered = jnp.where((lane >= 2) & (lane < 2 + STRIDE), inside, 0.0)
        pred_ref[t] = jnp.zeros(pred_ref.shape[1:], f32)
        for q in range(2):
            low, high = q * channels, (q + 1) * channels
            first = jnp.dot(table_ref[low:high, :], selector, preferred_element_type=f32)
            act = (jnp.maximum(first, 0.0) + jnp.log(1.0 + jnp.exp(-jnp.abs(first)))).astype(bf16).astype(f32)
            centered = act - column_mean(act)
            inverse_one = lax.rsqrt(column_mean(centered * centered) + EPSILON)
            hidden = centered * (inverse_one * inside)
            kept_ref[t, 2, low:high, :] = ((1.0 - jnp.exp(-act)) * (inverse_one * answered)).astype(bf16)
            stacked = with_neighbours(hidden)
            kept_ref[t, 0, low:high, :] = stacked[channels : 2 * channels]
            second = jnp.dot(kernel_ref[q], stacked, preferred_element_type=f32)
            small = jnp.exp(-jnp.abs(second))
            grown = 1.0 + small
            soft = jnp.maximum(second, 0.0) + jnp.log(grown)
            sigmoid = jnp.where(second >= 0.0, 1.0, small) / grown
            centered = soft - column_mean(soft)
            inverse_two = lax.rsqrt(column_mean(centered * centered) + EPSILON)
            normed = centered * inverse_two
            weights = weight_ref[q]
            weighted_mean = column_mean(normed * weights)
            pred_ref[t, q : q + 1, :] = weighted_mean * float(channels)
            factor = (weights - column_mean(weights) - normed * weighted_mean) * sigmoid
            kept_ref[t, 1, low:high, :] = (factor * (inverse_two * inside)).astype(bf16)
        pltpu.make_async_copy(kept_ref.at[t], far_ref.at[t], sems.at[t]).start()
        return carry

    def wait(t, carry):
        pltpu.make_async_copy(kept_ref.at[t], far_ref.at[t], sems.at[t]).wait()
        return carry

    tiles = tiles_of(count)
    lax.fori_loop(0, tiles, step, 0)
    lax.fori_loop(0, tiles, wait, 0)


def align_kernel(where_ref, spread_ref, pred_ref, own_ref, left_ref, right_ref, far_left_ref, far_right_ref, *refs):
    residual_ref, slot_refs, (window_ref, placed_ref) = refs[0], refs[1:6], refs[6:]
    frames = far_left_ref.shape[1]
    s, m = where_ref[0], where_ref[1]
    spread = spread_ref[...].astype(f32)
    seq = lax.broadcasted_iota(jnp.int32, spread.shape, 0)
    share = spread.shape[1] // 4
    owner = lax.shift_right_logical(lax.broadcasted_iota(jnp.int32, spread.shape, 1), share.bit_length() - 1)
    earlier = (seq < s) | ((seq == s) & (owner < m))
    before = jnp.sum(jnp.where(earlier, spread, 0.0)).astype(jnp.int32)
    total = jnp.sum(jnp.where((seq == s) & (owner == m), spread, 0.0))
    count = total.astype(jnp.int32)
    offset = before - (s - REACH) * frames
    window_ref[...] = jnp.zeros_like(window_ref)
    placed_ref[...] = jnp.zeros_like(placed_ref)
    for i, source in enumerate((far_left_ref, left_ref, own_ref, right_ref, far_right_ref)):
        window_ref[0:2, TILE + i * frames : TILE + (i + 1) * frames] = source[0:2, :]
    lane = lax.broadcasted_iota(jnp.int32, (8, TILE), 1)
    exact = (lane >= LEAD) & (lane < LEAD + STRIDE)

    def step(t, carry):
        at = jnp.clip(TILE + offset + t * STRIDE - LEAD, 0, window_ref.shape[1] - TILE - 128)
        rest = jnp.bitwise_and(at, 127)
        near = pl.ds(pl.multiple_of(at - rest, 128), TILE + 128)
        taken = pltpu.roll(window_ref[:, near], TILE + 128 - rest, 1)[:, 0:TILE]
        values = pred_ref[t]
        residual_ref[t] = values - taken
        own = exact & (lane + (t * STRIDE - LEAD) < count)
        moved = jnp.concatenate([jnp.where(own, values, 0.0), jnp.zeros((8, 128), f32)], axis=1)
        placed_ref[:, near] = placed_ref[:, near] + pltpu.roll(moved, rest, 1)
        return carry

    lax.fori_loop(0, tiles_of(total), step, 0)
    for i, slot in enumerate(slot_refs):
        slot[...] = placed_ref[0:2, TILE + i * frames : TILE + (i + 1) * frames]


def backward_kernel(
    last_seq,
    where_ref,
    own_ref,
    left_ref,
    right_ref,
    residual_ref,
    far_ref,
    conv_ref,
    out_ref,
    bounds_ref,
    sums_ref,
    kept_ref,
    sems,
):
    taps = conv_ref.shape[1]
    channels = conv_ref.shape[2]
    share = bounds_ref.shape[1]
    starts, ends, count, _, _ = share_bounds(where_ref, own_ref, left_ref, right_ref, last_seq, share, EDGE)
    tiles = tiles_of(count)

    def fetch(t, carry):
        pltpu.make_async_copy(far_ref.at[t], kept_ref.at[t], sems.at[t]).start()
        return carry

    lax.fori_loop(0, tiles, fetch, 0)
    bounds_ref[0] = jnp.broadcast_to(starts, (share, TILE))
    bounds_ref[1] = jnp.broadcast_to(ends, (share, TILE))
    sums_ref[...] = jnp.zeros_like(sums_ref)

    def step(t, carry):
        pltpu.make_async_copy(far_ref.at[t], kept_ref.at[t], sems.at[t]).wait()
        frames, _ = local_frames(t)
        selector = jnp.concatenate(
            [one_hot(frames + (k - 1.0), bounds_ref[0], bounds_ref[1]) for k in range(taps)], axis=0
        )
        for q in range(2):
            low, high = q * channels, (q + 1) * channels
            grad_second = kept_ref[t, 1, low:high, :].astype(f32) * residual_ref[t, q : q + 1, :]
            stacked = with_neighbours(grad_second)
            grad_hidden = jnp.zeros((channels, TILE), f32)
            for k in range(taps):
                part = stacked[(taps - 1 - k) * channels : (taps - k) * channels]
                grad_hidden = grad_hidden + jnp.dot(conv_ref[q, k], part, preferred_element_type=f32)
            normed = kept_ref[t, 0, low:high, :].astype(f32)
            first_mean = column_mean(grad_hidden)
            second_mean = column_mean(grad_hidden * normed)
            scale = kept_ref[t, 2, low:high, :].astype(f32)
            grad_first = (grad_hidden - first_mean - normed * second_mean) * scale
            sums_ref[:, low:high] += lax.dot_general(
                selector, grad_first.astype(bf16), (((1,), (1,)), ((), ())), preferred_element_type=f32
            )
        return carry

    lax.fori_loop(0, tiles, step, 0)
    out_ref[...] = sums_ref[...].astype(bf16)


def merge_kernel(sums_ref, own_ref, *refs):
    arrived, out_ref = refs[:-1], refs[-1]
    depth = sums_ref.shape[0]
    half = out_ref.shape[1]
    out_ref[0:depth, :] = sums_ref[...]
    left = own_ref[...]
    for source in arrived:
        left = left + source[...]
    parts = []
    for _ in range(3):
        part = left.astype(bf16).astype(f32)
        left = left - part
        parts += [part[:, 0:half], part[:, half : 2 * half]]
    parts.append(jnp.zeros((4, half), f32))
    out_ref[depth:, :] = jnp.concatenate(parts, axis=0).astype(bf16)


def finish_kernel(where_ref, *refs):
    merged_refs, slice_refs, (pred_ref, out_ref, rows_ref) = refs[:4], refs[4:8], refs[8:]
    taps = rows_ref.shape[0]
    chunk = slice_refs[0].shape[2]
    members = len(merged_refs)
    share = rows_ref.shape[1] // members
    depth = taps * share
    half = merged_refs[0].shape[1]
    pred = jnp.zeros((2, 2 * half), f32)
    for d, source in enumerate(merged_refs):
        owner = lax.rem(where_ref[1] + members - d, members)
        at = pl.ds(pl.multiple_of(owner * share, share), share)
        for k in range(taps):
            rows_ref[k, at, :] = source[k * share : (k + 1) * share, :]
        parts = source[depth:, :].astype(f32)
        for i in range(3):
            pred = pred + jnp.concatenate([parts[4 * i : 4 * i + 2], parts[4 * i + 2 : 4 * i + 4]], axis=1)
    pred_ref[...] = pred
    total = jnp.zeros(out_ref.shape, f32)
    for d, source in enumerate(slice_refs):
        owner = lax.rem(where_ref[1] + members - d, members)
        for k in range(taps):
            total = total + lax.dot_general(
                rows_ref[k, :, pl.ds(pl.multiple_of(owner * chunk, chunk), chunk)],
                source[k],
                (((1,), (1,)), ((), ())),
                preferred_element_type=f32,
            )
    out_ref[...] = total.astype(bf16)


def body(phoneme_rows, durations, conv_first, conv_second, readout, targets):
    seq_size = lax.axis_size("seq")
    members = lax.axis_size("mp")
    block, width = phoneme_rows.shape
    frames = targets.shape[1]
    taps, _, chunk = conv_first.shape
    channels = conv_second.shape[2]
    features = width // members
    share = block // members
    window = share + 2 * EDGE
    most = -(-(share * LONGEST + 2) // STRIDE)
    last_seq = seq_size - 1
    where = jnp.stack([lax.axis_index("seq"), lax.axis_index("mp")]).astype(jnp.int32)
    pack = jax.ShapeDtypeStruct((2 * HALO, width), f32)

    to_right, to_left, spread = call(
        pack_kernel,
        "pack",
        vmem=4,
        moved=2 * 32 * width,
        out_shape=(pack, pack, jax.ShapeDtypeStruct((seq_size, block), jnp.int32)),
        in_specs=[
            copied((1, block)),
            copied(targets.shape),
            pl.BlockSpec((16, width), lambda _: (0, 0)),
            pl.BlockSpec((16, width), lambda _: (block // 16 - 1, 0)),
        ],
        out_specs=(whole(),) * 3,
    )(in_hbm(durations.reshape(1, block)), in_hbm(targets), in_hbm(phoneme_rows), in_hbm(phoneme_rows))

    left = rotate(to_right, "seq", 1)
    right = rotate(to_left, "seq", -1)
    far_left = rotate(targets, "seq", 2)
    far_right = rotate(targets, "seq", -2)

    piece = jax.ShapeDtypeStruct((taps * window, chunk), bf16)
    conv_slice = jax.ShapeDtypeStruct((taps, features, chunk), bf16)
    pieces = call(
        rows_kernel,
        "row_products",
        vmem=8,
        flops=2 * block * width * taps * chunk,
        moved=2 * block * width + 2 * taps * width * chunk,
        out_shape=(piece,) * 4 + (conv_slice,) * 4,
        in_specs=[scalars(), copied(phoneme_rows.shape), whole(), whole(), copied(conv_first.shape)],
        out_specs=(whole(),) * 8,
        scratch_shapes=[VMEM((taps, block + 2 * EDGE, chunk), bf16)],
    )(where, in_hbm(phoneme_rows), left, right, in_hbm(conv_first))

    order = (1, 3, 2)
    tables = {0: pieces[0], **{d: rotate(pieces[d], "mp", d) for d in order}}
    slices = {0: pieces[4], **{d: rotate(pieces[4 + d], "mp", d) for d in order}}
    everyone = lax.all_to_all(spread, "seq", 0, 0, tiled=True)

    per_tile = 2 * channels * TILE
    kept_shape = (most, 3, 2 * channels, TILE)
    thin = jax.ShapeDtypeStruct((most, 8, TILE), f32)
    pred, kept = call(
        functools.partial(forward_kernel, last_seq),
        "forward",
        flops=2 * per_tile * 2 * (taps * window + taps * channels),
        moved=2 * per_tile * 6,
        out_shape=(thin, pltpu.HBM(kept_shape, bf16)),
        in_specs=[scalars()] + [whole()] * 7 + [copied(conv_second.shape), copied(readout.shape)],
        out_specs=(whole(), pl.BlockSpec(memory_space=pl.ANY)),
        scratch_shapes=[
            VMEM((2, window, TILE), f32),
            VMEM((2 * channels, taps * window), bf16),
            VMEM((2, channels, taps * channels), bf16),
            VMEM((2, channels, TILE), f32),
            VMEM(kept_shape, bf16),
            pltpu.SemaphoreType.DMA((most,)),
        ],
    )(where, to_right, left, right, *(tables[d] for d in range(4)), in_hbm(conv_second), in_hbm(readout))

    pred, slices = lax.optimization_barrier((pred, slices))
    slot = jax.ShapeDtypeStruct((2, frames), f32)
    reach = (2 * REACH + 1) * frames + 2 * TILE + 256
    residual, *slots = call(
        align_kernel,
        "align",
        vmem=4,
        moved=most * 8 * TILE * 8,
        out_shape=(thin,) + (slot,) * 5,
        in_specs=[scalars()] + [whole()] * 7,
        out_specs=(whole(),) * 6,
        scratch_shapes=[VMEM((8, reach), f32), VMEM((8, reach), f32)],
    )(where, everyone, pred, to_right, left, right, far_left, far_right)

    arrived = [rotate(slots[at], "seq", at - REACH) for at in (3, 1, 4, 0)]

    sums = call(
        functools.partial(backward_kernel, last_seq),
        "backward",
        flops=2 * per_tile * 2 * (taps * share + taps * channels),
        moved=2 * per_tile * 6,
        out_shape=jax.ShapeDtypeStruct((taps * share, 2 * channels), bf16),
        in_specs=[scalars()] + [whole()] * 4 + [pl.BlockSpec(memory_space=pl.ANY), copied(conv_second.shape)],
        out_specs=whole(),
        scratch_shapes=[
            VMEM((2, share, TILE), f32),
            VMEM((taps * share, 2 * channels), f32),
            VMEM(kept_shape, bf16),
            pltpu.SemaphoreType.DMA((most,)),
        ],
    )(where, to_right, left, right, residual, in_hbm(kept), in_hbm(conv_second))

    merged = call(
        merge_kernel,
        "merge",
        vmem=4,
        moved=taps * share * channels * 8,
        out_shape=jax.ShapeDtypeStruct((taps * share + 16, frames // 2), bf16),
        in_specs=[whole()] * 6,
        out_specs=whole(),
    )(sums, slots[REACH], *arrived)

    mergeds = {0: merged, **{d: rotate(merged, "mp", d) for d in order}}
    predicted, row_grad = call(
        finish_kernel,
        "finish",
        vmem=8,
        flops=2 * block * features * taps * 2 * channels,
        moved=8 * taps * features * chunk,
        out_shape=(slot, jax.ShapeDtypeStruct((block, features), bf16)),
        in_specs=[scalars()] + [whole()] * 8,
        out_specs=(copied((2, frames)), copied((block, features))),
        scratch_shapes=[VMEM((taps, block, 2 * channels), bf16)],
    )(where, *(mergeds[d] for d in range(4)), *(slices[d] for d in range(4)))
    return (predicted, row_grad)


def solution(mesh):
    in_specs = (P("seq", None), P("seq"), P(None, None, "mp"), P(), P(), P(None, "seq"))
    out_specs = (P(None, "seq"), P("seq", "mp"))
    return jax.shard_map(body, mesh=mesh, in_specs=in_specs, out_specs=out_specs, check_vma=False)
```

```python
import functools

import jax
import jax.numpy as jnp
from jax import lax
from jax.experimental import pallas as pl
from jax.experimental.pallas import tpu as pltpu
from jax.sharding import PartitionSpec as P

EPSILON = 1e-05
TILE = 256
STRIDE = 252
LEAD = 3
HALO = 4
EDGE = 16
LONGEST = 40
REACH = 2
f32 = jnp.float32
bf16 = jnp.bfloat16
VMEM = pltpu.VMEM
SMEM = pltpu.SMEM


def whole():
    return pl.BlockSpec(memory_space=VMEM)


def copied(shape):
    return pl.BlockSpec(shape, lambda _: (0,) * len(shape))


def in_hbm(array):
    return pltpu.with_memory_space_constraint(array, pltpu.HBM)


def scalars():
    return pl.BlockSpec(memory_space=SMEM)


def call(kernel, name, *, flops=0, moved=0, vmem=24, **kwargs):
    return pl.pallas_call(
        kernel,
        name=name,
        grid=(1,),
        cost_estimate=pl.CostEstimate(flops=flops, bytes_accessed=moved, transcendentals=0),
        compiler_params=pltpu.CompilerParams(vmem_limit_bytes=vmem * 1024 * 1024),
        **kwargs,
    )


def rotate(block, axis, distance):
    size = lax.axis_size(axis)
    return lax.ppermute(block, axis, [(i, (i + distance) % size) for i in range(size)])


def pack_kernel(dur_ref, targets_ref, head_ref, tail_ref, to_right_ref, to_left_ref, spread_ref):
    block = dur_ref.shape[1]
    frames = targets_ref.shape[1]
    dur = dur_ref[...]
    rows = (tail_ref[...].astype(f32)[16 - HALO : 16], head_ref[...].astype(f32)[0:HALO])
    for out, halo in zip((to_right_ref, to_left_ref), rows):
        out[...] = jnp.zeros_like(out)
        out[0:2, 0:frames] = targets_ref[...]
        out[2:3, 0:block] = dur.astype(f32)
        out[HALO : 2 * HALO, :] = halo
    spread_ref[...] = jnp.broadcast_to(dur, spread_ref.shape)


def prepare_kernel(where_ref, rows_ref, conv_ref, second_ref, readout_ref, products_ref, *refs):
    bundle_refs, (turned_ref, kernel_ref, weight_ref) = refs[:4], refs[4:]
    taps, width, _ = conv_ref.shape
    block = rows_ref.shape[0]
    channels = second_ref.shape[2]
    members = len(bundle_refs)
    features = width // members
    low = taps * (block // members + 2 * EDGE)
    for k in range(taps):
        product = jnp.dot(rows_ref[...], conv_ref[k], preferred_element_type=f32)
        products_ref[k * block : (k + 1) * block, :] = product.astype(bf16)
    for d in range(members):
        target = lax.rem(where_ref[1] + d, members)
        at = pl.ds(pl.multiple_of(target * features, features), features)
        for k in range(taps):
            bundle_refs[d][low + k * features : low + (k + 1) * features, :] = conv_ref[k, at, :]
    for q in range(2):
        for k in range(taps):
            turned_ref[q, :, k * channels : (k + 1) * channels] = second_ref[q, k].T
            kernel_ref[q, k] = second_ref[q, k]
    rows = jnp.concatenate([readout_ref[...].astype(f32), jnp.zeros((6, channels), f32)], axis=0)
    weight_ref[...] = rows.T


def split(values):
    terms = []
    for _ in range(3):
        terms.append(values.astype(bf16).astype(f32))
        values = values - terms[-1]
    return terms


def pieces_kernel(where_ref, products_ref, left_ref, right_ref, far_ref, *refs):
    given_refs, bundle_refs, (halo_ref, table_ref) = refs[:4], refs[4:8], refs[8:]
    channels = products_ref.shape[1]
    members = len(bundle_refs)
    features = halo_ref.shape[1] // members
    taps = table_ref.shape[0]
    block = products_ref.shape[0] // taps
    share = block // members
    window = share + 2 * EDGE
    low = taps * window
    high = low + taps * features
    halo_ref[...] = jnp.zeros_like(halo_ref)
    halo_ref[EDGE - HALO : EDGE, :] = left_ref[HALO : 2 * HALO]
    halo_ref[EDGE : EDGE + HALO, :] = right_ref[HALO : 2 * HALO]
    for k in range(taps):
        product = jnp.zeros((2 * EDGE, channels), f32)
        for d in range(members):
            owner = lax.rem(where_ref[1] + d, members)
            part = halo_ref[:, pl.ds(pl.multiple_of(owner * features, features), features)].astype(bf16)
            cut = given_refs[d][low + k * features : low + (k + 1) * features, :]
            product = product + jnp.dot(part, cut, preferred_element_type=f32)
        table_ref[k, 0:EDGE, :] = product[0:EDGE].astype(bf16)
        table_ref[k, EDGE : EDGE + block, :] = products_ref[k * block : (k + 1) * block, :]
        table_ref[k, EDGE + block :, :] = product[EDGE:].astype(bf16)
    far = far_ref[...]
    parts = [
        term[:, c * channels : (c + 1) * channels]
        for term in split(far)
        for c in range(far.shape[1] // channels)
    ]
    parts = jnp.concatenate(parts, axis=0).astype(bf16)
    for d in range(members):
        target = lax.rem(where_ref[1] + d, members)
        at = pl.ds(pl.multiple_of(target * share, share), window)
        for k in range(taps):
            bundle_refs[d][k * window : (k + 1) * window, :] = table_ref[k, at, :]
        bundle_refs[d][high:, :] = parts


def share_bounds(where_ref, own_ref, left_ref, right_ref, last_seq, rows, first_row):
    block = 4 * (rows - 2 * (EDGE - first_row))
    share = block // 4
    s, m = where_ref[0], where_ref[1]
    lane = lax.broadcasted_iota(jnp.int32, (1, block), 1)
    near = jnp.where((lane >= block - HALO) & (s > 0), left_ref[2:3, 0:block], 0.0)
    far = jnp.where((lane < HALO) & (s < last_seq), right_ref[2:3, 0:block], 0.0)
    own = own_ref[2:3, 0:block]
    durations = jnp.concatenate([near, own, far], axis=1)
    phoneme = lax.broadcasted_iota(jnp.int32, (1, 3 * block), 1) - block
    begin = m * share
    row = lax.broadcasted_iota(jnp.int32, (rows, 3 * block), 0) + (begin + first_row - EDGE)
    at = jnp.broadcast_to(phoneme, (rows, 3 * block))
    spread = jnp.broadcast_to(durations, (rows, 3 * block))
    later = at >= begin

    def bound(limit):
        signed = jnp.where(later & (at < limit), spread, 0.0) - jnp.where(
            (at < begin) & (at >= limit), spread, 0.0
        )
        return jnp.sum(signed, axis=1, keepdims=True)

    count = jnp.sum(jnp.where((phoneme >= begin) & (phoneme < begin + share), durations, 0.0))
    skipped = jnp.sum(jnp.where((phoneme >= 0) & (phoneme < begin), durations, 0.0))
    return bound(row), bound(row + 1), count, skipped, jnp.sum(own)


def tiles_of(count):
    return lax.div(count.astype(jnp.int32) + (2 + STRIDE - 1), STRIDE)


def one_hot(frames, starts, ends):
    return jnp.where((frames >= starts) & (frames < ends), 1.0, 0.0).astype(bf16)


def local_frames(t):
    lane = lax.broadcasted_iota(jnp.int32, (1, TILE), 1)
    return (lane + (t * STRIDE - LEAD)).astype(f32), lane


def column_mean(values):
    return jnp.sum(values, axis=0, keepdims=True) * (1.0 / values.shape[0])


def with_neighbours(values):
    return jnp.concatenate(
        [
            pltpu.roll(values, 1, 1).astype(bf16),
            values.astype(bf16),
            pltpu.roll(values, TILE - 1, 1).astype(bf16),
        ],
        axis=0,
    )


def forward_kernel(
    last_seq,
    where_ref,
    spread_ref,
    own_ref,
    left_ref,
    right_ref,
    far_ref,
    piece_ref,
    one_ref,
    two_ref,
    three_ref,
    kernel_ref,
    readout_ref,
    residual_ref,
    kept_ref,
    *refs,
):
    slot_refs, (bounds_ref, table_ref, weight_ref, pred_ref, window_ref, placed_ref) = refs[:5], refs[5:]
    channels = readout_ref.shape[0]
    chunk = piece_ref.shape[1]
    taps = kernel_ref.shape[2] // channels
    window = bounds_ref.shape[1]
    depth = taps * window
    members = 2 * channels // chunk
    frames_each = far_ref.shape[1]
    s, m = where_ref[0], where_ref[1]
    starts, ends, total, skipped, block_total = share_bounds(
        where_ref, own_ref, left_ref, right_ref, last_seq, window, 0
    )
    bounds_ref[0] = jnp.broadcast_to(starts, (window, TILE))
    bounds_ref[1] = jnp.broadcast_to(ends, (window, TILE))
    lowest = jnp.where(s == 0, -skipped, -1e9)
    end = jnp.where(s == last_seq, block_total - skipped, 1e9)
    for d, source in enumerate((piece_ref, one_ref, two_ref, three_ref)):
        owner = lax.rem(m + members - d, members)
        table_ref[pl.ds(pl.multiple_of(owner * chunk, chunk), chunk), :] = source[0:depth, :].T

    for q in range(2):
        weight_ref[q] = jnp.broadcast_to(readout_ref[:, q : q + 1], (channels, TILE))
    seq = lax.broadcasted_iota(jnp.int32, spread_ref.shape, 0)
    before = jnp.sum(jnp.where(seq < s, spread_ref[...].astype(f32), 0.0))
    count = total.astype(jnp.int32)
    offset = (before + skipped).astype(jnp.int32) - (s - REACH) * frames_each
    window_ref[...] = jnp.zeros_like(window_ref)
    placed_ref[...] = jnp.zeros_like(placed_ref)
    pred_ref[...] = jnp.zeros_like(pred_ref)
    parts = one_ref[one_ref.shape[0] - 3 * 2 * frames_each // chunk :, :].astype(f32)
    terms = [parts[i * 2 * frames_each // chunk : (i + 1) * 2 * frames_each // chunk] for i in range(3)]
    terms = terms[0] + terms[1] + terms[2]
    other = jnp.concatenate([terms[2 * c : 2 * c + 2] for c in range(frames_each // chunk)], axis=1)
    even = jnp.bitwise_and(m, 1) == 0
    here = far_ref[...]
    beside = (jnp.where(even, here, other), left_ref[0:2], own_ref[0:2], right_ref[0:2], jnp.where(even, other, here))
    for i, source in enumerate(beside):
        window_ref[0:2, TILE + i * frames_each : TILE + (i + 1) * frames_each] = source
    exact_lane = lax.broadcasted_iota(jnp.int32, (8, TILE), 1)
    exact = (exact_lane >= LEAD) & (exact_lane < LEAD + STRIDE)

    def step(t, carry):
        frames, lane = local_frames(t)
        selector = jnp.concatenate(
            [one_hot(frames + (k - 1.0), bounds_ref[0], bounds_ref[1]) for k in range(taps)], axis=0
        )
        inside = jnp.where((frames >= lowest) & (frames < end), 1.0, 0.0)
        answered = jnp.where((lane >= 2) & (lane < 2 + STRIDE), inside, 0.0)
        for q in range(2):
            low, high = q * channels, (q + 1) * channels
            first = jnp.dot(table_ref[low:high, :], selector, preferred_element_type=f32)
            act = (jnp.maximum(first, 0.0) + jnp.log(1.0 + jnp.exp(-jnp.abs(first)))).astype(bf16).astype(f32)
            centered = act - column_mean(act)
            inverse_one = lax.rsqrt(column_mean(centered * centered) + EPSILON)
            hidden = centered * (inverse_one * inside)
            kept_ref[t, 2, low:high, :] = ((1.0 - jnp.exp(-act)) * (inverse_one * answered)).astype(bf16)
            stacked = with_neighbours(hidden)
            kept_ref[t, 0, low:high, :] = stacked[channels : 2 * channels]
            second = jnp.dot(kernel_ref[q], stacked, preferred_element_type=f32)
            small = jnp.exp(-jnp.abs(second))
            grown = 1.0 + small
            soft = jnp.maximum(second, 0.0) + jnp.log(grown)
            sigmoid = jnp.where(second >= 0.0, 1.0, small) / grown
            centered = soft - column_mean(soft)
            inverse_two = lax.rsqrt(column_mean(centered * centered) + EPSILON)
            normed = centered * inverse_two
            weights = weight_ref[q]
            weighted_mean = column_mean(normed * weights)
            pred_ref[q : q + 1, :] = weighted_mean * float(channels)
            factor = (weights - column_mean(weights) - normed * weighted_mean) * sigmoid
            kept_ref[t, 1, low:high, :] = (factor * (inverse_two * inside)).astype(bf16)
        at = jnp.clip(TILE + offset + t * STRIDE - LEAD, 0, window_ref.shape[1] - TILE - 128)
        rest = jnp.bitwise_and(at, 127)
        near = pl.ds(pl.multiple_of(at - rest, 128), TILE + 128)
        taken = pltpu.roll(window_ref[:, near], TILE + 128 - rest, 1)[:, 0:TILE]
        values = pred_ref[...]
        residual_ref[t] = values - taken
        own = exact & (exact_lane + (t * STRIDE - LEAD) < count)
        moved = jnp.concatenate([jnp.where(own, values, 0.0), jnp.zeros((8, 128), f32)], axis=1)
        placed_ref[:, near] = placed_ref[:, near] + pltpu.roll(moved, rest, 1)
        return carry

    lax.fori_loop(0, tiles_of(total), step, 0)
    for i, slot in enumerate(slot_refs):
        slot[...] = placed_ref[0:2, TILE + i * frames_each : TILE + (i + 1) * frames_each]


def backward_kernel(
    last_seq,
    where_ref,
    own_ref,
    left_ref,
    right_ref,
    residual_ref,
    kept_ref,
    conv_ref,
    out_ref,
    bounds_ref,
    sums_ref,
):
    taps = conv_ref.shape[1]
    channels = conv_ref.shape[2]
    share = bounds_ref.shape[1]
    starts, ends, count, _, _ = share_bounds(where_ref, own_ref, left_ref, right_ref, last_seq, share, EDGE)
    tiles = tiles_of(count)
    bounds_ref[0] = jnp.broadcast_to(starts, (share, TILE))
    bounds_ref[1] = jnp.broadcast_to(ends, (share, TILE))
    sums_ref[...] = jnp.zeros_like(sums_ref)

    def step(t, carry):
        frames, _ = local_frames(t)
        selector = jnp.concatenate(
            [one_hot(frames + (k - 1.0), bounds_ref[0], bounds_ref[1]) for k in range(taps)], axis=0
        )
        for q in range(2):
            low, high = q * channels, (q + 1) * channels
            grad_second = kept_ref[t, 1, low:high, :].astype(f32) * residual_ref[t, q : q + 1, :]
            stacked = with_neighbours(grad_second)
            grad_hidden = jnp.zeros((channels, TILE), f32)
            for k in range(taps):
                part = stacked[(taps - 1 - k) * channels : (taps - k) * channels]
                grad_hidden = grad_hidden + jnp.dot(conv_ref[q, k], part, preferred_element_type=f32)
            normed = kept_ref[t, 0, low:high, :].astype(f32)
            first_mean = column_mean(grad_hidden)
            second_mean = column_mean(grad_hidden * normed)
            scale = kept_ref[t, 2, low:high, :].astype(f32)
            grad_first = (grad_hidden - first_mean - normed * second_mean) * scale
            sums_ref[:, low:high] += lax.dot_general(
                selector, grad_first.astype(bf16), (((1,), (1,)), ((), ())), preferred_element_type=f32
            )
        return carry

    lax.fori_loop(0, tiles, step, 0)
    out_ref[...] = sums_ref[...].astype(bf16)


def merge_kernel(sums_ref, own_ref, *refs):
    arrived, out_ref = refs[:-1], refs[-1]
    depth = sums_ref.shape[0]
    half = out_ref.shape[1]
    out_ref[0:depth, :] = sums_ref[...]
    left = own_ref[...]
    for source in arrived:
        left = left + source[...]
    parts = [term[:, i * half : (i + 1) * half] for term in split(left) for i in range(2)]
    parts.append(jnp.zeros((4, half), f32))
    out_ref[depth:, :] = jnp.concatenate(parts, axis=0).astype(bf16)


def finish_kernel(where_ref, *refs):
    merged_refs, bundle_refs, (pred_ref, out_ref, rows_ref) = refs[:4], refs[4:8], refs[8:]
    taps = rows_ref.shape[0]
    chunk = bundle_refs[0].shape[1]
    features = out_ref.shape[1]
    members = len(merged_refs)
    low = taps * (rows_ref.shape[1] // members + 2 * EDGE)
    share = rows_ref.shape[1] // members
    depth = taps * share
    half = merged_refs[0].shape[1]
    pred = jnp.zeros((2, 2 * half), f32)
    for d, source in enumerate(merged_refs):
        owner = lax.rem(where_ref[1] + members - d, members)
        at = pl.ds(pl.multiple_of(owner * share, share), share)
        for k in range(taps):
            rows_ref[k, at, :] = source[k * share : (k + 1) * share, :]
        parts = source[depth:, :].astype(f32)
        for i in range(3):
            pred = pred + jnp.concatenate([parts[4 * i : 4 * i + 2], parts[4 * i + 2 : 4 * i + 4]], axis=1)
    pred_ref[...] = pred
    total = jnp.zeros(out_ref.shape, f32)
    for d, source in enumerate(bundle_refs):
        owner = lax.rem(where_ref[1] + members - d, members)
        for k in range(taps):
            total = total + lax.dot_general(
                rows_ref[k, :, pl.ds(pl.multiple_of(owner * chunk, chunk), chunk)],
                source[low + k * features : low + (k + 1) * features, :],
                (((1,), (1,)), ((), ())),
                preferred_element_type=f32,
            )
    out_ref[...] = total.astype(bf16)


def body(phoneme_rows, durations, conv_first, conv_second, readout, targets):
    seq_size = lax.axis_size("seq")
    members = lax.axis_size("mp")
    block, width = phoneme_rows.shape
    frames = targets.shape[1]
    taps, _, chunk = conv_first.shape
    channels = conv_second.shape[2]
    features = width // members
    share = block // members
    window = share + 2 * EDGE
    most = -(-(share * LONGEST + 2) // STRIDE)
    last_seq = seq_size - 1
    where = jnp.stack([lax.axis_index("seq"), lax.axis_index("mp")]).astype(jnp.int32)
    pack = jax.ShapeDtypeStruct((2 * HALO, width), f32)

    to_right, to_left, spread = call(
        pack_kernel,
        "pack",
        vmem=4,
        moved=2 * 32 * width,
        out_shape=(pack, pack, jax.ShapeDtypeStruct((seq_size, block), jnp.int32)),
        in_specs=[
            copied((1, block)),
            copied(targets.shape),
            pl.BlockSpec((16, width), lambda _: (0, 0)),
            pl.BlockSpec((16, width), lambda _: (block // 16 - 1, 0)),
        ],
        out_specs=(whole(),) * 3,
    )(in_hbm(durations.reshape(1, block)), in_hbm(targets), in_hbm(phoneme_rows), in_hbm(phoneme_rows))

    left = rotate(to_right, "seq", 1)
    right = rotate(to_left, "seq", -1)
    far = lax.ppermute(
        targets,
        ("seq", "mp"),
        [
            ((s + (-REACH if m % 2 == 0 else REACH)) % seq_size * members + m, s * members + m)
            for s in range(seq_size)
            for m in range(members)
        ],
    )

    bundle = jax.ShapeDtypeStruct((taps * (window + features) + 3 * 2 * frames // chunk, chunk), bf16)
    products, *made = call(
        prepare_kernel,
        "prepare",
        vmem=12,
        flops=2 * block * width * taps * chunk,
        moved=2 * block * width + 2 * taps * width * chunk + 4 * taps * channels * channels,
        out_shape=(jax.ShapeDtypeStruct((taps * block, chunk), bf16),)
        + (bundle,) * 4
        + (
            jax.ShapeDtypeStruct((2, channels, taps * channels), bf16),
            jax.ShapeDtypeStruct(conv_second.shape, bf16),
            jax.ShapeDtypeStruct((channels, 8), f32),
        ),
        in_specs=[
            scalars(),
            copied(phoneme_rows.shape),
            copied(conv_first.shape),
            copied(conv_second.shape),
            copied(readout.shape),
        ],
        out_specs=(whole(),) * 8,
    )(where, in_hbm(phoneme_rows), in_hbm(conv_first), in_hbm(conv_second), in_hbm(readout))
    bundles, (turned, kernel, weight) = made[:4], made[4:]

    bundles = call(
        pieces_kernel,
        "pieces",
        vmem=8,
        flops=2 * 2 * EDGE * width * taps * chunk,
        moved=2 * taps * width * chunk,
        out_shape=(bundle,) * 4,
        in_specs=[scalars()] + [whole()] * 8,
        out_specs=(whole(),) * 4,
        input_output_aliases={5 + d: d for d in range(4)},
        scratch_shapes=[VMEM((2 * EDGE, width), f32), VMEM((taps, block + 2 * EDGE, chunk), bf16)],
    )(where, products, left, right, far, *bundles)

    order = (1, 3, 2)
    everyone = lax.all_to_all(spread, "seq", 0, 0, tiled=True)
    bundles = [bundles[0], *(rotate(bundles[d], "mp", d) for d in order)]

    per_tile = 2 * channels * TILE
    thin = jax.ShapeDtypeStruct((most, 8, TILE), f32)
    slot = jax.ShapeDtypeStruct((2, frames), f32)
    reach = (2 * REACH + 1) * frames + 2 * TILE + 256
    residual, kept, *slots = call(
        functools.partial(forward_kernel, last_seq),
        "forward",
        flops=2 * per_tile * 2 * (taps * window + taps * channels),
        moved=2 * per_tile * 6,
        out_shape=(thin, jax.ShapeDtypeStruct((most, 3, 2 * channels, TILE), bf16)) + (slot,) * 5,
        in_specs=[scalars()] + [whole()] * 11,
        out_specs=(whole(),) * 7,
        scratch_shapes=[
            VMEM((2, window, TILE), f32),
            VMEM((2 * channels, taps * window), bf16),
            VMEM((2, channels, TILE), f32),
            VMEM((8, TILE), f32),
            VMEM((8, reach), f32),
            VMEM((8, reach), f32),
        ],
    )(where, everyone, to_right, left, right, far, bundles[0], bundles[1], bundles[3], bundles[2], turned, weight)

    arrived = [rotate(slots[at], "seq", at - REACH) for at in (3, 1, 4, 0)]

    sums = call(
        functools.partial(backward_kernel, last_seq),
        "backward",
        flops=2 * per_tile * 2 * (taps * share + taps * channels),
        moved=2 * per_tile * 6,
        out_shape=jax.ShapeDtypeStruct((taps * share, 2 * channels), bf16),
        in_specs=[scalars()] + [whole()] * 6,
        out_specs=whole(),
        scratch_shapes=[VMEM((2, share, TILE), f32), VMEM((taps * share, 2 * channels), f32)],
    )(where, to_right, left, right, residual, kept, kernel)

    merged = call(
        merge_kernel,
        "merge",
        vmem=4,
        moved=taps * share * channels * 8,
        out_shape=jax.ShapeDtypeStruct((taps * share + 16, frames // 2), bf16),
        in_specs=[whole()] * 6,
        out_specs=whole(),
    )(sums, slots[REACH], *arrived)

    mergeds = [merged, *(rotate(merged, "mp", d) for d in order)]
    predicted, row_grad = call(
        finish_kernel,
        "finish",
        vmem=8,
        flops=2 * block * features * taps * 2 * channels,
        moved=8 * taps * features * chunk,
        out_shape=(slot, jax.ShapeDtypeStruct((block, features), bf16)),
        in_specs=[scalars()] + [whole()] * 8,
        out_specs=(copied((2, frames)), copied((block, features))),
        scratch_shapes=[VMEM((taps, block, 2 * channels), bf16)],
    )(where, *(mergeds[i] for i in (0, 1, 3, 2)), *(bundles[i] for i in (0, 1, 3, 2)))
    return (predicted, row_grad)


def solution(mesh):
    in_specs = (P("seq", None), P("seq"), P(None, None, "mp"), P(), P(), P(None, "seq"))
    out_specs = (P(None, "seq"), P("seq", "mp"))
    return jax.shard_map(body, mesh=mesh, in_specs=in_specs, out_specs=out_specs, check_vma=False)
```

```python
import functools

import jax
import jax.numpy as jnp
from jax import lax
from jax.experimental import pallas as pl
from jax.experimental.pallas import tpu as pltpu
from jax.sharding import PartitionSpec as P

EPSILON = 1e-05
TILE = 256
STRIDE = 252
LEAD = 3
HALO = 4
EDGE = 16
LONGEST = 40
REACH = 2
NEAR = 2
f32 = jnp.float32
bf16 = jnp.bfloat16
VMEM = pltpu.VMEM
SMEM = pltpu.SMEM


def whole():
    return pl.BlockSpec(memory_space=VMEM)


def copied(shape):
    return pl.BlockSpec(shape, lambda _: (0,) * len(shape))


def in_hbm(array):
    return pltpu.with_memory_space_constraint(array, pltpu.HBM)


def scalars():
    return pl.BlockSpec(memory_space=SMEM)


def call(kernel, name, *, flops=0, moved=0, vmem=24, **kwargs):
    return pl.pallas_call(
        kernel,
        name=name,
        grid=(1,),
        cost_estimate=pl.CostEstimate(flops=flops, bytes_accessed=moved, transcendentals=0),
        compiler_params=pltpu.CompilerParams(vmem_limit_bytes=vmem * 1024 * 1024),
        **kwargs,
    )


def rotate(block, axis, distance):
    size = lax.axis_size(axis)
    return lax.ppermute(block, axis, [(i, (i + distance) % size) for i in range(size)])


def pack_kernel(where_ref, dur_ref, targets_ref, readout_ref, head_ref, tail_ref, to_mate_ref, to_outer_ref):
    block = dur_ref.shape[1]
    frames = targets_ref.shape[1]
    channels = readout_ref.shape[1]
    even = jnp.bitwise_and(where_ref[0], 1) == 0
    tail = tail_ref[...].astype(f32)[16 - HALO : 16]
    head = head_ref[...].astype(f32)[0:HALO]
    rows = (jnp.where(even, tail, head), jnp.where(even, head, tail))
    readout = readout_ref[...].astype(f32)
    for out, halo in zip((to_mate_ref, to_outer_ref), rows):
        out[...] = jnp.zeros_like(out)
        out[0:2, 0:frames] = targets_ref[...]
        out[2:3, 0:block] = dur_ref[...].astype(f32)
        for q in range(2):
            out[3:4, q * channels : (q + 1) * channels] = readout[q : q + 1]
        out[HALO : 2 * HALO, :] = halo


def prepare_kernel(where_ref, dur_ref, rows_ref, conv_ref, second_ref, spread_ref, products_ref, *refs):
    bundle_refs, (turned_ref, wide_ref, sem) = refs[:4], refs[4:]
    wide_ref[...] = jnp.broadcast_to(dur_ref[...], wide_ref.shape)
    spread = pltpu.make_async_copy(wide_ref, spread_ref, sem)
    spread.start()
    taps, width, _ = conv_ref.shape
    block = rows_ref.shape[0]
    channels = second_ref.shape[2]
    members = len(bundle_refs)
    features = width // members
    low = taps * (block // members + 2 * EDGE)
    for k in range(taps):
        product = jnp.dot(rows_ref[...], conv_ref[k], preferred_element_type=f32)
        products_ref[k * block : (k + 1) * block, :] = product.astype(bf16)
    for d in range(members):
        target = lax.rem(where_ref[1] + d, members)
        at = pl.ds(pl.multiple_of(target * features, features), features)
        for k in range(taps):
            bundle_refs[d][low + k * features : low + (k + 1) * features, :] = conv_ref[k, at, :]
    for q in range(2):
        for k in range(taps):
            turned_ref[q, :, k * channels : (k + 1) * channels] = second_ref[q, k].T
    spread.wait()


def split(values):
    terms = []
    for _ in range(3):
        terms.append(values.astype(bf16).astype(f32))
        values = values - terms[-1]
    return terms


def pieces_kernel(where_ref, products_ref, mate_ref, outer_ref, far_ref, *refs):
    given_refs, bundle_refs, (left_ref, right_ref, halo_ref, table_ref) = refs[:4], refs[4:8], refs[8:]
    even = jnp.bitwise_and(where_ref[0], 1) == 0
    left_ref[...] = jnp.where(even, outer_ref[...], mate_ref[...])
    right_ref[...] = jnp.where(even, mate_ref[...], outer_ref[...])
    channels = products_ref.shape[1]
    members = len(bundle_refs)
    features = halo_ref.shape[1] // members
    taps = table_ref.shape[0]
    block = products_ref.shape[0] // taps
    share = block // members
    window = share + 2 * EDGE
    low = taps * window
    high = low + taps * features
    halo_ref[...] = jnp.zeros_like(halo_ref)
    halo_ref[EDGE - HALO : EDGE, :] = left_ref[HALO : 2 * HALO]
    halo_ref[EDGE : EDGE + HALO, :] = right_ref[HALO : 2 * HALO]
    for k in range(taps):
        product = jnp.zeros((2 * EDGE, channels), f32)
        for d in range(members):
            owner = lax.rem(where_ref[1] + d, members)
            part = halo_ref[:, pl.ds(pl.multiple_of(owner * features, features), features)].astype(bf16)
            cut = given_refs[d][low + k * features : low + (k + 1) * features, :]
            product = product + jnp.dot(part, cut, preferred_element_type=f32)
        table_ref[k, 0:EDGE, :] = product[0:EDGE].astype(bf16)
        table_ref[k, EDGE : EDGE + block, :] = products_ref[k * block : (k + 1) * block, :]
        table_ref[k, EDGE + block :, :] = product[EDGE:].astype(bf16)
    far = far_ref[...]
    parts = [
        term[:, c * channels : (c + 1) * channels]
        for term in split(far)
        for c in range(far.shape[1] // channels)
    ]
    parts = jnp.concatenate(parts, axis=0).astype(bf16)
    for d in range(members):
        target = lax.rem(where_ref[1] + d, members)
        at = pl.ds(pl.multiple_of(target * share, share), window)
        for k in range(taps):
            bundle_refs[d][k * window : (k + 1) * window, :] = table_ref[k, at, :]
        bundle_refs[d][high:, :] = parts


def share_bounds(where_ref, own_ref, left_ref, right_ref, last_seq, rows, first_row):
    block = 4 * (rows - 2 * (EDGE - first_row))
    share = block // 4
    s, m = where_ref[0], where_ref[1]
    lane = lax.broadcasted_iota(jnp.int32, (1, block), 1)
    near = jnp.where((lane >= block - HALO) & (s > 0), left_ref[2:3, 0:block], 0.0)
    far = jnp.where((lane < HALO) & (s < last_seq), right_ref[2:3, 0:block], 0.0)
    own = own_ref[2:3, 0:block]
    durations = jnp.concatenate([near, own, far], axis=1)
    phoneme = lax.broadcasted_iota(jnp.int32, (1, 3 * block), 1) - block
    begin = m * share
    row = lax.broadcasted_iota(jnp.int32, (rows, 3 * block), 0) + (begin + first_row - EDGE)
    at = jnp.broadcast_to(phoneme, (rows, 3 * block))
    spread = jnp.broadcast_to(durations, (rows, 3 * block))
    later = at >= begin

    def bound(limit):
        signed = jnp.where(later & (at < limit), spread, 0.0) - jnp.where(
            (at < begin) & (at >= limit), spread, 0.0
        )
        return jnp.sum(signed, axis=1, keepdims=True)

    count = jnp.sum(jnp.where((phoneme >= begin) & (phoneme < begin + share), durations, 0.0))
    skipped = jnp.sum(jnp.where((phoneme >= 0) & (phoneme < begin), durations, 0.0))
    return bound(row), bound(row + 1), count, skipped, jnp.sum(own)


def tiles_of(count):
    return lax.div(count.astype(jnp.int32) + (2 + STRIDE - 1), STRIDE)


def one_hot(frames, starts, ends):
    return jnp.where((frames >= starts) & (frames < ends), 1.0, 0.0).astype(bf16)


def local_frames(t):
    lane = lax.broadcasted_iota(jnp.int32, (1, TILE), 1)
    return (lane + (t * STRIDE - LEAD)).astype(f32), lane


def column_mean(values):
    return jnp.sum(values, axis=0, keepdims=True) * (1.0 / values.shape[0])


def with_neighbours(values):
    return jnp.concatenate(
        [
            pltpu.roll(values, 1, 1).astype(bf16),
            values.astype(bf16),
            pltpu.roll(values, TILE - 1, 1).astype(bf16),
        ],
        axis=0,
    )


def forward_kernel(
    last_seq,
    where_ref,
    own_ref,
    left_ref,
    right_ref,
    piece_ref,
    one_ref,
    two_ref,
    three_ref,
    kernel_ref,
    pred_ref,
    offset_ref,
    near_ref,
    far_kept_ref,
    bounds_ref,
    table_ref,
    weight_ref,
    more_ref,
    sems,
):
    channels = kernel_ref.shape[1]
    chunk = piece_ref.shape[1]
    taps = kernel_ref.shape[2] // channels
    window = bounds_ref.shape[1]
    depth = taps * window
    members = 2 * channels // chunk
    s, m = where_ref[0], where_ref[1]
    starts, ends, total, skipped, block_total = share_bounds(
        where_ref, own_ref, left_ref, right_ref, last_seq, window, 0
    )
    bounds_ref[0] = jnp.broadcast_to(starts, (window, TILE))
    bounds_ref[1] = jnp.broadcast_to(ends, (window, TILE))
    lowest = jnp.where(s == 0, -skipped, -1e9)
    end = jnp.where(s == last_seq, block_total - skipped, 1e9)
    for q in range(2):
        column = own_ref[:, q * channels : (q + 1) * channels].T
        weight_ref[q] = jnp.broadcast_to(column[:, 3:4], (channels, TILE))
    for d, source in enumerate((piece_ref, one_ref, two_ref, three_ref)):
        owner = lax.rem(m + members - d, members)
        table_ref[pl.ds(pl.multiple_of(owner * chunk, chunk), chunk), :] = source[0:depth, :].T

    for q in range(2):
        column = own_ref[:, q * channels : (q + 1) * channels].T
        weight_ref[q] = jnp.broadcast_to(column[:, 3:4], (channels, TILE))
    offset_ref[0] = skipped.astype(jnp.int32)
    offset_ref[1] = total.astype(jnp.int32)
    pred_ref[...] = jnp.zeros_like(pred_ref)

    def work(t, kept_ref, at):
        frames, lane = local_frames(t)
        selector = jnp.concatenate(
            [one_hot(frames + (k - 1.0), bounds_ref[0], bounds_ref[1]) for k in range(taps)], axis=0
        )
        inside = jnp.where((frames >= lowest) & (frames < end), 1.0, 0.0)
        answered = jnp.where((lane >= 2) & (lane < 2 + STRIDE), inside, 0.0)
        for q in range(2):
            low, high = q * channels, (q + 1) * channels
            first = jnp.dot(table_ref[low:high, :], selector, preferred_element_type=f32)
            act = (jnp.maximum(first, 0.0) + jnp.log(1.0 + jnp.exp(-jnp.abs(first)))).astype(bf16).astype(f32)
            centered = act - column_mean(act)
            inverse_one = lax.rsqrt(column_mean(centered * centered) + EPSILON)
            hidden = centered * (inverse_one * inside)
            kept_ref[at, q, 2] = ((1.0 - jnp.exp(-act)) * (inverse_one * answered)).astype(bf16)
            stacked = with_neighbours(hidden)
            kept_ref[at, q, 0] = stacked[channels : 2 * channels]
            second = jnp.dot(kernel_ref[q], stacked, preferred_element_type=f32)
            small = jnp.exp(-jnp.abs(second))
            soft = jnp.maximum(second, 0.0) + jnp.log(1.0 + small)
            sigmoid = jnp.exp(second - soft)
            centered = soft - column_mean(soft)
            inverse_two = lax.rsqrt(column_mean(centered * centered) + EPSILON)
            normed = centered * inverse_two
            weights = weight_ref[q]
            weighted_mean = column_mean(normed * weights)
            pred_ref[t, q : q + 1, :] = weighted_mean * float(channels)
            factor = (weights - column_mean(weights) - normed * weighted_mean) * sigmoid
            kept_ref[at, q, 1] = (factor * (inverse_two * inside)).astype(bf16)

    def step(t, carry):
        work(t, near_ref, t)
        return carry

    def far_step(t, carry):
        work(t, more_ref, t - NEAR)
        pltpu.make_async_copy(more_ref.at[t - NEAR], far_kept_ref.at[t - NEAR], sems.at[t - NEAR]).start()
        return carry

    def wait(t, carry):
        pltpu.make_async_copy(more_ref.at[t - NEAR], far_kept_ref.at[t - NEAR], sems.at[t - NEAR]).wait()
        return carry

    tiles = tiles_of(total)
    lax.fori_loop(0, jnp.minimum(tiles, NEAR), step, 0)
    lax.fori_loop(NEAR, tiles, far_step, 0)
    lax.fori_loop(NEAR, tiles, wait, 0)


def align_kernel(
    where_ref,
    offset_ref,
    spread_ref,
    pred_ref,
    own_ref,
    left_ref,
    right_ref,
    far_ref,
    one_ref,
    far_kept_ref,
    residual_ref,
    kept_ref,
    *refs,
):
    slot_refs, (window_ref, placed_ref, sems) = refs[:5], refs[5:]
    s, m = where_ref[0], where_ref[1]
    chunk = one_ref.shape[1]
    frames_each = far_ref.shape[1]
    count = offset_ref[1]
    tiles = lax.div(count + (2 + STRIDE - 1), STRIDE)

    def fetch(t, carry):
        pltpu.make_async_copy(far_kept_ref.at[t - NEAR], kept_ref.at[t - NEAR], sems.at[t - NEAR]).start()
        return carry

    def wait(t, carry):
        pltpu.make_async_copy(far_kept_ref.at[t - NEAR], kept_ref.at[t - NEAR], sems.at[t - NEAR]).wait()
        return carry

    lax.fori_loop(NEAR, tiles, fetch, 0)
    seq = lax.broadcasted_iota(jnp.int32, spread_ref.shape, 0)
    before = jnp.sum(jnp.where(seq < s, spread_ref[...].astype(f32), 0.0))
    offset = before.astype(jnp.int32) + offset_ref[0] - (s - REACH) * frames_each
    window_ref[...] = jnp.zeros_like(window_ref)
    placed_ref[...] = jnp.zeros_like(placed_ref)
    parts = one_ref[one_ref.shape[0] - 3 * 2 * frames_each // chunk :, :].astype(f32)
    terms = [parts[i * 2 * frames_each // chunk : (i + 1) * 2 * frames_each // chunk] for i in range(3)]
    terms = terms[0] + terms[1] + terms[2]
    other = jnp.concatenate([terms[2 * c : 2 * c + 2] for c in range(frames_each // chunk)], axis=1)
    even = jnp.bitwise_and(m, 1) == 0
    here = far_ref[...]
    beside = (jnp.where(even, here, other), left_ref[0:2], own_ref[0:2], right_ref[0:2], jnp.where(even, other, here))
    for i, source in enumerate(beside):
        window_ref[0:2, TILE + i * frames_each : TILE + (i + 1) * frames_each] = source
    exact_lane = lax.broadcasted_iota(jnp.int32, (2, TILE), 1)
    exact = (exact_lane >= LEAD) & (exact_lane < LEAD + STRIDE)

    def step(t, carry):
        at = jnp.clip(TILE + offset + t * STRIDE - LEAD, 0, window_ref.shape[1] - TILE - 128)
        rest = jnp.bitwise_and(at, 127)
        near = pl.ds(pl.multiple_of(at - rest, 128), TILE + 128)
        taken = pltpu.roll(window_ref[:, near], TILE + 128 - rest, 1)[0:2, 0:TILE]
        values = pred_ref[t]
        residual_ref[t] = values - taken
        own = exact & (exact_lane + (t * STRIDE - LEAD) < count)
        moved = jnp.concatenate([jnp.where(own, values, 0.0), jnp.zeros((2, 128), f32)], axis=1)
        moved = jnp.concatenate([moved, jnp.zeros((6, TILE + 128), f32)], axis=0)
        placed_ref[:, near] = placed_ref[:, near] + pltpu.roll(moved, rest, 1)
        return carry

    lax.fori_loop(0, tiles, step, 0)
    even = jnp.bitwise_and(s, 1) == 0
    slots = [placed_ref[0:2, TILE + i * frames_each : TILE + (i + 1) * frames_each] for i in range(5)]
    slots[1], slots[3] = jnp.where(even, slots[1], slots[3]), jnp.where(even, slots[3], slots[1])
    for slot, values in zip(slot_refs, slots):
        slot[...] = values
    lax.fori_loop(NEAR, tiles, wait, 0)


def backward_kernel(
    last_seq,
    where_ref,
    own_ref,
    left_ref,
    right_ref,
    residual_ref,
    near_ref,
    more_ref,
    turned_ref,
    out_ref,
    bounds_ref,
    sums_ref,
    conv_ref,
):
    taps = conv_ref.shape[1]
    channels = conv_ref.shape[2]
    share = bounds_ref.shape[1]
    starts, ends, count, _, _ = share_bounds(where_ref, own_ref, left_ref, right_ref, last_seq, share, EDGE)
    bounds_ref[0] = jnp.broadcast_to(starts, (share, TILE))
    bounds_ref[1] = jnp.broadcast_to(ends, (share, TILE))
    sums_ref[...] = jnp.zeros_like(sums_ref)
    for q in range(2):
        for k in range(taps):
            conv_ref[q, k] = turned_ref[q, :, k * channels : (k + 1) * channels].T

    def work(t, kept_ref, at):
        frames, _ = local_frames(t)
        selector = jnp.concatenate(
            [one_hot(frames + (k - 1.0), bounds_ref[0], bounds_ref[1]) for k in range(taps)], axis=0
        )
        for q in range(2):
            low, high = q * channels, (q + 1) * channels
            grad_second = kept_ref[at, q, 1].astype(f32) * residual_ref[t, q : q + 1, :]
            stacked = with_neighbours(grad_second)
            grad_hidden = jnp.zeros((channels, TILE), f32)
            for k in range(taps):
                part = stacked[(taps - 1 - k) * channels : (taps - k) * channels]
                grad_hidden = grad_hidden + jnp.dot(conv_ref[q, k], part, preferred_element_type=f32)
            normed = kept_ref[at, q, 0].astype(f32)
            first_mean = column_mean(grad_hidden)
            second_mean = column_mean(grad_hidden * normed)
            scale = kept_ref[at, q, 2].astype(f32)
            grad_first = (grad_hidden - first_mean - normed * second_mean) * scale
            sums_ref[:, low:high] += lax.dot_general(
                selector, grad_first.astype(bf16), (((1,), (1,)), ((), ())), preferred_element_type=f32
            )

    def step(t, carry):
        work(t, near_ref, t)
        return carry

    def far_step(t, carry):
        work(t, more_ref, t - NEAR)
        return carry

    tiles = tiles_of(count)
    lax.fori_loop(0, jnp.minimum(tiles, NEAR), step, 0)
    lax.fori_loop(NEAR, tiles, far_step, 0)
    out_ref[...] = sums_ref[...].astype(bf16)


def merge_kernel(sums_ref, own_ref, *refs):
    arrived, out_ref = refs[:-1], refs[-1]
    depth = sums_ref.shape[0]
    half = out_ref.shape[1]
    out_ref[0:depth, :] = sums_ref[...]
    left = own_ref[...]
    for source in arrived:
        left = left + source[...]
    parts = [term[:, i * half : (i + 1) * half] for term in split(left) for i in range(2)]
    parts.append(jnp.zeros((4, half), f32))
    out_ref[depth:, :] = jnp.concatenate(parts, axis=0).astype(bf16)


def finish_kernel(where_ref, *refs):
    merged_refs, bundle_refs, (pred_ref, out_ref, rows_ref) = refs[:4], refs[4:8], refs[8:]
    taps = rows_ref.shape[0]
    chunk = bundle_refs[0].shape[1]
    features = out_ref.shape[1]
    members = len(merged_refs)
    low = taps * (rows_ref.shape[1] // members + 2 * EDGE)
    share = rows_ref.shape[1] // members
    depth = taps * share
    half = merged_refs[0].shape[1]
    pred = jnp.zeros((2, 2 * half), f32)
    for d, source in enumerate(merged_refs):
        owner = lax.rem(where_ref[1] + members - d, members)
        at = pl.ds(pl.multiple_of(owner * share, share), share)
        for k in range(taps):
            rows_ref[k, at, :] = source[k * share : (k + 1) * share, :]
        parts = source[depth:, :].astype(f32)
        for i in range(3):
            pred = pred + jnp.concatenate([parts[4 * i : 4 * i + 2], parts[4 * i + 2 : 4 * i + 4]], axis=1)
    pred_ref[...] = pred
    total = jnp.zeros(out_ref.shape, f32)
    for pair in (0, 2):
        owners = [lax.rem(where_ref[1] + members - d, members) for d in (pair, pair + 1)]
        sources = bundle_refs[pair : pair + 2]
        for k in range(taps):
            rows = [rows_ref[k, :, pl.ds(pl.multiple_of(owner * chunk, chunk), chunk)] for owner in owners]
            cuts = [source[low + k * features : low + (k + 1) * features, :] for source in sources]
            total = total + lax.dot_general(
                jnp.concatenate(rows, axis=1),
                jnp.concatenate(cuts, axis=1),
                (((1,), (1,)), ((), ())),
                preferred_element_type=f32,
            )
    out_ref[...] = total.astype(bf16)


def body(phoneme_rows, durations, conv_first, conv_second, readout, targets):
    seq_size = lax.axis_size("seq")
    members = lax.axis_size("mp")
    block, width = phoneme_rows.shape
    frames = targets.shape[1]
    taps, _, chunk = conv_first.shape
    channels = conv_second.shape[2]
    features = width // members
    share = block // members
    window = share + 2 * EDGE
    most = -(-(share * LONGEST + 2) // STRIDE)
    last_seq = seq_size - 1
    where = jnp.stack([lax.axis_index("seq"), lax.axis_index("mp")]).astype(jnp.int32)
    anywhere = pl.BlockSpec(memory_space=pl.ANY)
    pack = jax.ShapeDtypeStruct((2 * HALO, width), f32)
    dur = durations.reshape(1, block)

    to_mate, to_outer = call(
        pack_kernel,
        "pack",
        vmem=4,
        moved=2 * 32 * width,
        out_shape=(pack, pack),
        in_specs=[
            scalars(),
            copied((1, block)),
            copied(targets.shape),
            copied(readout.shape),
            pl.BlockSpec((16, width), lambda _: (0, 0)),
            pl.BlockSpec((16, width), lambda _: (block // 16 - 1, 0)),
        ],
        out_specs=(whole(),) * 2,
    )(where, in_hbm(dur), in_hbm(targets), in_hbm(readout), in_hbm(phoneme_rows), in_hbm(phoneme_rows))

    def outer_of(s):
        return (s + (1 if s % 2 else -1)) % seq_size

    from_mate = lax.ppermute(to_mate, "seq", [(s, s ^ 1) for s in range(seq_size)])
    from_outer = lax.ppermute(to_outer, "seq", [(s, outer_of(s)) for s in range(seq_size)])
    far = lax.ppermute(
        targets,
        ("seq", "mp"),
        [
            ((s + (-REACH if m % 2 == 0 else REACH)) % seq_size * members + m, s * members + m)
            for s in range(seq_size)
            for m in range(members)
        ],
    )

    bundle = jax.ShapeDtypeStruct((taps * (window + features) + 3 * 2 * frames // chunk, chunk), bf16)
    spread, products, *made = call(
        prepare_kernel,
        "prepare",
        vmem=12,
        flops=2 * block * width * taps * chunk,
        moved=2 * block * width + 2 * taps * width * chunk + 4 * taps * channels * channels,
        out_shape=(pltpu.HBM((seq_size, block), jnp.int32), jax.ShapeDtypeStruct((taps * block, chunk), bf16))
        + (bundle,) * 4
        + (jax.ShapeDtypeStruct((2, channels, taps * channels), bf16),),
        in_specs=[
            scalars(),
            copied((1, block)),
            copied(phoneme_rows.shape),
            copied(conv_first.shape),
            copied(conv_second.shape),
        ],
        out_specs=(anywhere,) + (whole(),) * 6,
        scratch_shapes=[VMEM((seq_size, block), jnp.int32), pltpu.SemaphoreType.DMA],
    )(where, in_hbm(dur), in_hbm(phoneme_rows), in_hbm(conv_first), in_hbm(conv_second))
    bundles, turned = made[:4], made[4]

    *bundles, left, right = call(
        pieces_kernel,
        "pieces",
        vmem=8,
        flops=2 * 2 * EDGE * width * taps * chunk,
        moved=2 * taps * width * chunk,
        out_shape=(bundle,) * 4 + (pack,) * 2,
        in_specs=[scalars()] + [whole()] * 8,
        out_specs=(whole(),) * 6,
        input_output_aliases={5 + d: d for d in range(4)},
        scratch_shapes=[VMEM((2 * EDGE, width), f32), VMEM((taps, block + 2 * EDGE, chunk), bf16)],
    )(where, products, from_mate, from_outer, far, *bundles)

    order = (1, 3, 2)
    everyone = lax.all_to_all(spread, "seq", 0, 0, tiled=True)
    bundles = [bundles[0], *(rotate(bundles[d], "mp", d) for d in order)]

    per_tile = 2 * channels * TILE
    thin = jax.ShapeDtypeStruct((most, 2, TILE), f32)
    slot = jax.ShapeDtypeStruct((2, frames), f32)
    reach = (2 * REACH + 1) * frames + 2 * TILE + 256
    near_shape = (NEAR, 2, 3, channels, TILE)
    far_shape = (most - NEAR, 2, 3, channels, TILE)
    ordered = [bundles[i] for i in (0, 1, 3, 2)]
    pred, offset, near, kept = call(
        functools.partial(forward_kernel, last_seq),
        "forward",
        flops=2 * per_tile * 2 * (taps * window + taps * channels),
        moved=2 * per_tile * 6,
        out_shape=(
            thin,
            jax.ShapeDtypeStruct((2,), jnp.int32),
            jax.ShapeDtypeStruct(near_shape, bf16),
            pltpu.HBM(far_shape, bf16),
        ),
        in_specs=[scalars()] + [whole()] * 8,
        out_specs=(whole(), scalars(), whole(), anywhere),
        scratch_shapes=[
            VMEM((2, window, TILE), f32),
            VMEM((2 * channels, taps * window), bf16),
            VMEM((2, channels, TILE), f32),
            VMEM(far_shape, bf16),
            pltpu.SemaphoreType.DMA((most - NEAR,)),
        ],
    )(where, to_mate, left, right, *ordered, turned)

    residual, kept, *slots = call(
        align_kernel,
        "align",
        vmem=4,
        moved=most * 8 * TILE * 8,
        out_shape=(thin, jax.ShapeDtypeStruct(far_shape, bf16)) + (slot,) * 5,
        in_specs=[scalars(), scalars()] + [whole()] * 7 + [anywhere],
        out_specs=(whole(),) * 7,
        scratch_shapes=[
            VMEM((8, reach), f32),
            VMEM((8, reach), f32),
            pltpu.SemaphoreType.DMA((most - NEAR,)),
        ],
    )(where, offset, everyone, pred, to_mate, left, right, far, bundles[1], in_hbm(kept))

    arrived = [
        lax.ppermute(slots[3], "seq", [(s, s ^ 1) for s in range(seq_size)]),
        lax.ppermute(slots[1], "seq", [(s, outer_of(s)) for s in range(seq_size)]),
        rotate(slots[4], "seq", REACH),
        rotate(slots[0], "seq", -REACH),
    ]

    sums = call(
        functools.partial(backward_kernel, last_seq),
        "backward",
        flops=2 * per_tile * 2 * (taps * share + taps * channels),
        moved=2 * per_tile * 6,
        out_shape=jax.ShapeDtypeStruct((taps * share, 2 * channels), bf16),
        in_specs=[scalars()] + [whole()] * 7,
        out_specs=whole(),
        scratch_shapes=[
            VMEM((2, share, TILE), f32),
            VMEM((taps * share, 2 * channels), f32),
            VMEM(conv_second.shape, bf16),
        ],
    )(where, to_mate, left, right, residual, near, kept, turned)

    merged = call(
        merge_kernel,
        "merge",
        vmem=4,
        moved=taps * share * channels * 8,
        out_shape=jax.ShapeDtypeStruct((taps * share + 16, frames // 2), bf16),
        in_specs=[whole()] * 6,
        out_specs=whole(),
    )(sums, slots[REACH], *arrived)

    mergeds = [merged, *(rotate(merged, "mp", d) for d in order)]
    predicted, row_grad = call(
        finish_kernel,
        "finish",
        vmem=8,
        flops=2 * block * features * taps * 2 * channels,
        moved=8 * taps * features * chunk,
        out_shape=(slot, jax.ShapeDtypeStruct((block, features), bf16)),
        in_specs=[scalars()] + [whole()] * 8,
        out_specs=(copied((2, frames)), copied((block, features))),
        scratch_shapes=[VMEM((taps, block, 2 * channels), bf16)],
    )(where, *(mergeds[i] for i in (0, 1, 3, 2)), *ordered)
    return (predicted, row_grad)


def solution(mesh):
    in_specs = (P("seq", None), P("seq"), P(None, None, "mp"), P(), P(), P(None, "seq"))
    out_specs = (P(None, "seq"), P("seq", "mp"))
    return jax.shard_map(body, mesh=mesh, in_specs=in_specs, out_specs=out_specs, check_vma=False)
```

```python
import functools

import jax
import jax.numpy as jnp
from jax import lax
from jax.experimental import pallas as pl
from jax.experimental.pallas import tpu as pltpu
from jax.sharding import PartitionSpec as P

EPSILON = 1e-05
TILE = 512
STRIDE = 508
LEAD = 3
HALO = 4
EDGE = 16
LONGEST = 40
REACH = 2
NEAR = 1
f32 = jnp.float32
bf16 = jnp.bfloat16
VMEM = pltpu.VMEM
SMEM = pltpu.SMEM


def whole():
    return pl.BlockSpec(memory_space=VMEM)


def copied(shape):
    return pl.BlockSpec(shape, lambda _: (0,) * len(shape))


def in_hbm(array):
    return pltpu.with_memory_space_constraint(array, pltpu.HBM)


def scalars():
    return pl.BlockSpec(memory_space=SMEM)


def call(kernel, name, *, flops=0, moved=0, vmem=24, **kwargs):
    return pl.pallas_call(
        kernel,
        name=name,
        grid=(1,),
        cost_estimate=pl.CostEstimate(flops=flops, bytes_accessed=moved, transcendentals=0),
        compiler_params=pltpu.CompilerParams(vmem_limit_bytes=vmem * 1024 * 1024),
        **kwargs,
    )


def rotate(block, axis, distance):
    size = lax.axis_size(axis)
    return lax.ppermute(block, axis, [(i, (i + distance) % size) for i in range(size)])


def pack_kernel(where_ref, dur_ref, targets_ref, readout_ref, head_ref, tail_ref, to_mate_ref, to_outer_ref):
    block = dur_ref.shape[1]
    frames = targets_ref.shape[1]
    channels = readout_ref.shape[1]
    even = jnp.bitwise_and(where_ref[0], 1) == 0
    tail = tail_ref[...].astype(f32)[16 - HALO : 16]
    head = head_ref[...].astype(f32)[0:HALO]
    rows = (jnp.where(even, tail, head), jnp.where(even, head, tail))
    readout = readout_ref[...].astype(f32)
    for out, halo in zip((to_mate_ref, to_outer_ref), rows):
        out[...] = jnp.zeros_like(out)
        out[0:2, 0:frames] = targets_ref[...]
        out[2:3, 0:block] = dur_ref[...].astype(f32)
        for q in range(2):
            out[3:4, q * channels : (q + 1) * channels] = readout[q : q + 1]
        out[HALO : 2 * HALO, :] = halo


def prepare_kernel(where_ref, dur_ref, rows_ref, conv_ref, second_ref, spread_ref, products_ref, *refs):
    bundle_refs, (turned_ref, wide_ref, sem) = refs[:4], refs[4:]
    wide_ref[...] = jnp.broadcast_to(dur_ref[...], wide_ref.shape)
    spread = pltpu.make_async_copy(wide_ref, spread_ref, sem)
    spread.start()
    taps, width, _ = conv_ref.shape
    block = rows_ref.shape[0]
    channels = second_ref.shape[2]
    members = len(bundle_refs)
    features = width // members
    low = taps * (block // members + 2 * EDGE)
    for k in range(taps):
        product = jnp.dot(rows_ref[...], conv_ref[k], preferred_element_type=f32)
        products_ref[k * block : (k + 1) * block, :] = product.astype(bf16)
    for d in range(members):
        target = lax.rem(where_ref[1] + d, members)
        at = pl.ds(pl.multiple_of(target * features, features), features)
        for k in range(taps):
            bundle_refs[d][low + k * features : low + (k + 1) * features, :] = conv_ref[k, at, :]
    for q in range(2):
        for k in range(taps):
            turned_ref[q, :, k * channels : (k + 1) * channels] = second_ref[q, k].T
    spread.wait()


def split(values):
    terms = []
    for _ in range(3):
        terms.append(values.astype(bf16).astype(f32))
        values = values - terms[-1]
    return terms


def pieces_kernel(where_ref, products_ref, mate_ref, outer_ref, far_ref, *refs):
    given_refs, bundle_refs, (left_ref, right_ref, halo_ref, table_ref) = refs[:4], refs[4:8], refs[8:]
    even = jnp.bitwise_and(where_ref[0], 1) == 0
    left_ref[...] = jnp.where(even, outer_ref[...], mate_ref[...])
    right_ref[...] = jnp.where(even, mate_ref[...], outer_ref[...])
    channels = products_ref.shape[1]
    members = len(bundle_refs)
    features = halo_ref.shape[1] // members
    taps = table_ref.shape[0]
    block = products_ref.shape[0] // taps
    share = block // members
    window = share + 2 * EDGE
    low = taps * window
    high = low + taps * features
    halo_ref[...] = jnp.zeros_like(halo_ref)
    halo_ref[EDGE - HALO : EDGE, :] = left_ref[HALO : 2 * HALO]
    halo_ref[EDGE : EDGE + HALO, :] = right_ref[HALO : 2 * HALO]
    for k in range(taps):
        product = jnp.zeros((2 * EDGE, channels), f32)
        for d in range(members):
            owner = lax.rem(where_ref[1] + d, members)
            part = halo_ref[:, pl.ds(pl.multiple_of(owner * features, features), features)].astype(bf16)
            cut = given_refs[d][low + k * features : low + (k + 1) * features, :]
            product = product + jnp.dot(part, cut, preferred_element_type=f32)
        table_ref[k, 0:EDGE, :] = product[0:EDGE].astype(bf16)
        table_ref[k, EDGE : EDGE + block, :] = products_ref[k * block : (k + 1) * block, :]
        table_ref[k, EDGE + block :, :] = product[EDGE:].astype(bf16)
    far = far_ref[...]
    parts = [
        term[:, c * channels : (c + 1) * channels]
        for term in split(far)
        for c in range(far.shape[1] // channels)
    ]
    parts = jnp.concatenate(parts, axis=0).astype(bf16)
    for d in range(members):
        target = lax.rem(where_ref[1] + d, members)
        at = pl.ds(pl.multiple_of(target * share, share), window)
        for k in range(taps):
            bundle_refs[d][k * window : (k + 1) * window, :] = table_ref[k, at, :]
        bundle_refs[d][high:, :] = parts


def share_bounds(where_ref, own_ref, left_ref, right_ref, last_seq, rows, first_row):
    block = 4 * (rows - 2 * (EDGE - first_row))
    share = block // 4
    s, m = where_ref[0], where_ref[1]
    lane = lax.broadcasted_iota(jnp.int32, (1, block), 1)
    near = jnp.where((lane >= block - HALO) & (s > 0), left_ref[2:3, 0:block], 0.0)
    far = jnp.where((lane < HALO) & (s < last_seq), right_ref[2:3, 0:block], 0.0)
    own = own_ref[2:3, 0:block]
    durations = jnp.concatenate([near, own, far], axis=1)
    phoneme = lax.broadcasted_iota(jnp.int32, (1, 3 * block), 1) - block
    begin = m * share
    row = lax.broadcasted_iota(jnp.int32, (rows, 3 * block), 0) + (begin + first_row - EDGE)
    at = jnp.broadcast_to(phoneme, (rows, 3 * block))
    spread = jnp.broadcast_to(durations, (rows, 3 * block))
    later = at >= begin

    def bound(limit):
        signed = jnp.where(later & (at < limit), spread, 0.0) - jnp.where(
            (at < begin) & (at >= limit), spread, 0.0
        )
        return jnp.sum(signed, axis=1, keepdims=True)

    count = jnp.sum(jnp.where((phoneme >= begin) & (phoneme < begin + share), durations, 0.0))
    skipped = jnp.sum(jnp.where((phoneme >= 0) & (phoneme < begin), durations, 0.0))
    return bound(row), bound(row + 1), count, skipped, jnp.sum(own)


def tiles_of(count):
    return lax.div(count.astype(jnp.int32) + (2 + STRIDE - 1), STRIDE)


def one_hot(frames, starts, ends):
    return jnp.where((frames >= starts) & (frames < ends), 1.0, 0.0).astype(bf16)


def local_frames(t):
    lane = lax.broadcasted_iota(jnp.int32, (1, TILE), 1)
    return (lane + (t * STRIDE - LEAD)).astype(f32), lane


def column_mean(values):
    return jnp.sum(values, axis=0, keepdims=True) * (1.0 / values.shape[0])


def with_neighbours(values):
    return jnp.concatenate(
        [
            pltpu.roll(values, 1, 1).astype(bf16),
            values.astype(bf16),
            pltpu.roll(values, TILE - 1, 1).astype(bf16),
        ],
        axis=0,
    )


def forward_kernel(
    last_seq,
    where_ref,
    own_ref,
    left_ref,
    right_ref,
    piece_ref,
    one_ref,
    two_ref,
    three_ref,
    kernel_ref,
    pred_ref,
    offset_ref,
    near_ref,
    far_kept_ref,
    bounds_ref,
    table_ref,
    weight_ref,
    more_ref,
    sems,
):
    channels = kernel_ref.shape[1]
    chunk = piece_ref.shape[1]
    taps = kernel_ref.shape[2] // channels
    window = bounds_ref.shape[1]
    depth = taps * window
    members = 2 * channels // chunk
    s, m = where_ref[0], where_ref[1]
    starts, ends, total, skipped, block_total = share_bounds(
        where_ref, own_ref, left_ref, right_ref, last_seq, window, 0
    )
    bounds_ref[0] = jnp.broadcast_to(starts, (window, TILE))
    bounds_ref[1] = jnp.broadcast_to(ends, (window, TILE))
    lowest = jnp.where(s == 0, -skipped, -1e9)
    end = jnp.where(s == last_seq, block_total - skipped, 1e9)
    for q in range(2):
        column = own_ref[:, q * channels : (q + 1) * channels].T
        weight_ref[q] = jnp.broadcast_to(column[:, 3:4], (channels, TILE))
    for d, source in enumerate((piece_ref, one_ref, two_ref, three_ref)):
        owner = lax.rem(m + members - d, members)
        table_ref[pl.ds(pl.multiple_of(owner * chunk, chunk), chunk), :] = source[0:depth, :].T

    for q in range(2):
        column = own_ref[:, q * channels : (q + 1) * channels].T
        weight_ref[q] = jnp.broadcast_to(column[:, 3:4], (channels, TILE))
    offset_ref[0] = skipped.astype(jnp.int32)
    offset_ref[1] = total.astype(jnp.int32)
    pred_ref[...] = jnp.zeros_like(pred_ref)

    def work(t, kept_ref, at):
        frames, lane = local_frames(t)
        selector = jnp.concatenate(
            [one_hot(frames + (k - 1.0), bounds_ref[0], bounds_ref[1]) for k in range(taps)], axis=0
        )
        inside = jnp.where((frames >= lowest) & (frames < end), 1.0, 0.0)
        answered = jnp.where((lane >= 2) & (lane < 2 + STRIDE), inside, 0.0)
        for q in range(2):
            low, high = q * channels, (q + 1) * channels
            first = jnp.dot(table_ref[low:high, :], selector, preferred_element_type=f32)
            act = (jnp.maximum(first, 0.0) + jnp.log(1.0 + jnp.exp(-jnp.abs(first)))).astype(bf16).astype(f32)
            centered = act - column_mean(act)
            inverse_one = lax.rsqrt(column_mean(centered * centered) + EPSILON)
            hidden = centered * (inverse_one * inside)
            kept_ref[at, q, 2] = ((1.0 - jnp.exp(-act)) * (inverse_one * answered)).astype(bf16)
            stacked = with_neighbours(hidden)
            kept_ref[at, q, 0] = stacked[channels : 2 * channels]
            second = jnp.dot(kernel_ref[q], stacked, preferred_element_type=f32)
            small = jnp.exp(-jnp.abs(second))
            soft = jnp.maximum(second, 0.0) + jnp.log(1.0 + small)
            sigmoid = jnp.exp(second - soft)
            centered = soft - column_mean(soft)
            inverse_two = lax.rsqrt(column_mean(centered * centered) + EPSILON)
            normed = centered * inverse_two
            weights = weight_ref[q]
            weighted_mean = column_mean(normed * weights)
            pred_ref[t, q : q + 1, :] = weighted_mean * float(channels)
            factor = (weights - column_mean(weights) - normed * weighted_mean) * sigmoid
            kept_ref[at, q, 1] = (factor * (inverse_two * inside)).astype(bf16)

    def step(t, carry):
        work(t, near_ref, t)
        return carry

    def far_step(t, carry):
        work(t, more_ref, t - NEAR)
        pltpu.make_async_copy(more_ref.at[t - NEAR], far_kept_ref.at[t - NEAR], sems.at[t - NEAR]).start()
        return carry

    def wait(t, carry):
        pltpu.make_async_copy(more_ref.at[t - NEAR], far_kept_ref.at[t - NEAR], sems.at[t - NEAR]).wait()
        return carry

    tiles = tiles_of(total)
    lax.fori_loop(0, jnp.minimum(tiles, NEAR), step, 0)
    lax.fori_loop(NEAR, tiles, far_step, 0)
    lax.fori_loop(NEAR, tiles, wait, 0)


def align_kernel(
    where_ref,
    offset_ref,
    spread_ref,
    pred_ref,
    own_ref,
    left_ref,
    right_ref,
    far_ref,
    one_ref,
    far_kept_ref,
    residual_ref,
    kept_ref,
    *refs,
):
    slot_refs, (window_ref, placed_ref, sems) = refs[:5], refs[5:]
    s, m = where_ref[0], where_ref[1]
    chunk = one_ref.shape[1]
    frames_each = far_ref.shape[1]
    count = offset_ref[1]
    tiles = lax.div(count + (2 + STRIDE - 1), STRIDE)

    def fetch(t, carry):
        pltpu.make_async_copy(far_kept_ref.at[t - NEAR], kept_ref.at[t - NEAR], sems.at[t - NEAR]).start()
        return carry

    def wait(t, carry):
        pltpu.make_async_copy(far_kept_ref.at[t - NEAR], kept_ref.at[t - NEAR], sems.at[t - NEAR]).wait()
        return carry

    lax.fori_loop(NEAR, tiles, fetch, 0)
    seq = lax.broadcasted_iota(jnp.int32, spread_ref.shape, 0)
    before = jnp.sum(jnp.where(seq < s, spread_ref[...].astype(f32), 0.0))
    offset = before.astype(jnp.int32) + offset_ref[0] - (s - REACH) * frames_each
    window_ref[...] = jnp.zeros_like(window_ref)
    placed_ref[...] = jnp.zeros_like(placed_ref)
    parts = one_ref[one_ref.shape[0] - 3 * 2 * frames_each // chunk :, :].astype(f32)
    terms = [parts[i * 2 * frames_each // chunk : (i + 1) * 2 * frames_each // chunk] for i in range(3)]
    terms = terms[0] + terms[1] + terms[2]
    other = jnp.concatenate([terms[2 * c : 2 * c + 2] for c in range(frames_each // chunk)], axis=1)
    even = jnp.bitwise_and(m, 1) == 0
    here = far_ref[...]
    beside = (jnp.where(even, here, other), left_ref[0:2], own_ref[0:2], right_ref[0:2], jnp.where(even, other, here))
    for i, source in enumerate(beside):
        window_ref[0:2, TILE + i * frames_each : TILE + (i + 1) * frames_each] = source
    exact_lane = lax.broadcasted_iota(jnp.int32, (2, TILE), 1)
    exact = (exact_lane >= LEAD) & (exact_lane < LEAD + STRIDE)

    def step(t, carry):
        at = jnp.clip(TILE + offset + t * STRIDE - LEAD, 0, window_ref.shape[1] - TILE - 128)
        rest = jnp.bitwise_and(at, 127)
        near = pl.ds(pl.multiple_of(at - rest, 128), TILE + 128)
        taken = pltpu.roll(window_ref[:, near], TILE + 128 - rest, 1)[0:2, 0:TILE]
        values = pred_ref[t]
        residual_ref[t] = values - taken
        own = exact & (exact_lane + (t * STRIDE - LEAD) < count)
        moved = jnp.concatenate([jnp.where(own, values, 0.0), jnp.zeros((2, 128), f32)], axis=1)
        moved = jnp.concatenate([moved, jnp.zeros((6, TILE + 128), f32)], axis=0)
        placed_ref[:, near] = placed_ref[:, near] + pltpu.roll(moved, rest, 1)
        return carry

    lax.fori_loop(0, tiles, step, 0)
    even = jnp.bitwise_and(s, 1) == 0
    slots = [placed_ref[0:2, TILE + i * frames_each : TILE + (i + 1) * frames_each] for i in range(5)]
    slots[1], slots[3] = jnp.where(even, slots[1], slots[3]), jnp.where(even, slots[3], slots[1])
    for slot, values in zip(slot_refs, slots):
        slot[...] = values
    lax.fori_loop(NEAR, tiles, wait, 0)


def backward_kernel(
    last_seq,
    where_ref,
    own_ref,
    left_ref,
    right_ref,
    residual_ref,
    near_ref,
    more_ref,
    turned_ref,
    out_ref,
    bounds_ref,
    sums_ref,
    conv_ref,
):
    taps = conv_ref.shape[1]
    channels = conv_ref.shape[2]
    share = bounds_ref.shape[1]
    starts, ends, count, _, _ = share_bounds(where_ref, own_ref, left_ref, right_ref, last_seq, share, EDGE)
    bounds_ref[0] = jnp.broadcast_to(starts, (share, TILE))
    bounds_ref[1] = jnp.broadcast_to(ends, (share, TILE))
    sums_ref[...] = jnp.zeros_like(sums_ref)
    for q in range(2):
        for k in range(taps):
            conv_ref[q, k] = turned_ref[q, :, k * channels : (k + 1) * channels].T

    def work(t, kept_ref, at):
        frames, _ = local_frames(t)
        selector = jnp.concatenate(
            [one_hot(frames + (k - 1.0), bounds_ref[0], bounds_ref[1]) for k in range(taps)], axis=0
        )
        for q in range(2):
            low, high = q * channels, (q + 1) * channels
            grad_second = kept_ref[at, q, 1].astype(f32) * residual_ref[t, q : q + 1, :]
            stacked = with_neighbours(grad_second)
            grad_hidden = jnp.zeros((channels, TILE), f32)
            for k in range(taps):
                part = stacked[(taps - 1 - k) * channels : (taps - k) * channels]
                grad_hidden = grad_hidden + jnp.dot(conv_ref[q, k], part, preferred_element_type=f32)
            normed = kept_ref[at, q, 0].astype(f32)
            first_mean = column_mean(grad_hidden)
            second_mean = column_mean(grad_hidden * normed)
            scale = kept_ref[at, q, 2].astype(f32)
            grad_first = (grad_hidden - first_mean - normed * second_mean) * scale
            sums_ref[:, low:high] += lax.dot_general(
                selector, grad_first.astype(bf16), (((1,), (1,)), ((), ())), preferred_element_type=f32
            )

    def step(t, carry):
        work(t, near_ref, t)
        return carry

    def far_step(t, carry):
        work(t, more_ref, t - NEAR)
        return carry

    tiles = tiles_of(count)
    lax.fori_loop(0, jnp.minimum(tiles, NEAR), step, 0)
    lax.fori_loop(NEAR, tiles, far_step, 0)
    out_ref[...] = sums_ref[...].astype(bf16)


def merge_kernel(sums_ref, own_ref, *refs):
    arrived, out_ref = refs[:-1], refs[-1]
    depth = sums_ref.shape[0]
    half = out_ref.shape[1]
    out_ref[0:depth, :] = sums_ref[...]
    left = own_ref[...]
    for source in arrived:
        left = left + source[...]
    parts = [term[:, i * half : (i + 1) * half] for term in split(left) for i in range(2)]
    parts.append(jnp.zeros((4, half), f32))
    out_ref[depth:, :] = jnp.concatenate(parts, axis=0).astype(bf16)


def finish_kernel(where_ref, *refs):
    merged_refs, bundle_refs, (pred_ref, out_ref, rows_ref) = refs[:4], refs[4:8], refs[8:]
    taps = rows_ref.shape[0]
    chunk = bundle_refs[0].shape[1]
    features = out_ref.shape[1]
    members = len(merged_refs)
    low = taps * (rows_ref.shape[1] // members + 2 * EDGE)
    share = rows_ref.shape[1] // members
    depth = taps * share
    half = merged_refs[0].shape[1]
    pred = jnp.zeros((2, 2 * half), f32)
    for d, source in enumerate(merged_refs):
        owner = lax.rem(where_ref[1] + members - d, members)
        at = pl.ds(pl.multiple_of(owner * share, share), share)
        for k in range(taps):
            rows_ref[k, at, :] = source[k * share : (k + 1) * share, :]
        parts = source[depth:, :].astype(f32)
        for i in range(3):
            pred = pred + jnp.concatenate([parts[4 * i : 4 * i + 2], parts[4 * i + 2 : 4 * i + 4]], axis=1)
    pred_ref[...] = pred
    total = jnp.zeros(out_ref.shape, f32)
    for pair in (0, 2):
        owners = [lax.rem(where_ref[1] + members - d, members) for d in (pair, pair + 1)]
        sources = bundle_refs[pair : pair + 2]
        for k in range(taps):
            rows = [rows_ref[k, :, pl.ds(pl.multiple_of(owner * chunk, chunk), chunk)] for owner in owners]
            cuts = [source[low + k * features : low + (k + 1) * features, :] for source in sources]
            total = total + lax.dot_general(
                jnp.concatenate(rows, axis=1),
                jnp.concatenate(cuts, axis=1),
                (((1,), (1,)), ((), ())),
                preferred_element_type=f32,
            )
    out_ref[...] = total.astype(bf16)


def body(phoneme_rows, durations, conv_first, conv_second, readout, targets):
    seq_size = lax.axis_size("seq")
    members = lax.axis_size("mp")
    block, width = phoneme_rows.shape
    frames = targets.shape[1]
    taps, _, chunk = conv_first.shape
    channels = conv_second.shape[2]
    features = width // members
    share = block // members
    window = share + 2 * EDGE
    most = -(-(share * LONGEST + 2) // STRIDE)
    last_seq = seq_size - 1
    where = jnp.stack([lax.axis_index("seq"), lax.axis_index("mp")]).astype(jnp.int32)
    anywhere = pl.BlockSpec(memory_space=pl.ANY)
    pack = jax.ShapeDtypeStruct((2 * HALO, width), f32)
    dur = durations.reshape(1, block)

    to_mate, to_outer = call(
        pack_kernel,
        "pack",
        vmem=4,
        moved=2 * 32 * width,
        out_shape=(pack, pack),
        in_specs=[
            scalars(),
            copied((1, block)),
            copied(targets.shape),
            copied(readout.shape),
            pl.BlockSpec((16, width), lambda _: (0, 0)),
            pl.BlockSpec((16, width), lambda _: (block // 16 - 1, 0)),
        ],
        out_specs=(whole(),) * 2,
    )(where, in_hbm(dur), in_hbm(targets), in_hbm(readout), in_hbm(phoneme_rows), in_hbm(phoneme_rows))

    def outer_of(s):
        return (s + (1 if s % 2 else -1)) % seq_size

    from_mate = lax.ppermute(to_mate, "seq", [(s, s ^ 1) for s in range(seq_size)])
    from_outer = lax.ppermute(to_outer, "seq", [(s, outer_of(s)) for s in range(seq_size)])
    far = lax.ppermute(
        targets,
        ("seq", "mp"),
        [
            ((s + (-REACH if m % 2 == 0 else REACH)) % seq_size * members + m, s * members + m)
            for s in range(seq_size)
            for m in range(members)
        ],
    )

    bundle = jax.ShapeDtypeStruct((taps * (window + features) + 3 * 2 * frames // chunk, chunk), bf16)
    spread, products, *made = call(
        prepare_kernel,
        "prepare",
        vmem=12,
        flops=2 * block * width * taps * chunk,
        moved=2 * block * width + 2 * taps * width * chunk + 4 * taps * channels * channels,
        out_shape=(pltpu.HBM((seq_size, block), jnp.int32), jax.ShapeDtypeStruct((taps * block, chunk), bf16))
        + (bundle,) * 4
        + (jax.ShapeDtypeStruct((2, channels, taps * channels), bf16),),
        in_specs=[
            scalars(),
            copied((1, block)),
            copied(phoneme_rows.shape),
            copied(conv_first.shape),
            copied(conv_second.shape),
        ],
        out_specs=(anywhere,) + (whole(),) * 6,
        scratch_shapes=[VMEM((seq_size, block), jnp.int32), pltpu.SemaphoreType.DMA],
    )(where, in_hbm(dur), in_hbm(phoneme_rows), in_hbm(conv_first), in_hbm(conv_second))
    bundles, turned = made[:4], made[4]

    *bundles, left, right = call(
        pieces_kernel,
        "pieces",
        vmem=8,
        flops=2 * 2 * EDGE * width * taps * chunk,
        moved=2 * taps * width * chunk,
        out_shape=(bundle,) * 4 + (pack,) * 2,
        in_specs=[scalars()] + [whole()] * 8,
        out_specs=(whole(),) * 6,
        input_output_aliases={5 + d: d for d in range(4)},
        scratch_shapes=[VMEM((2 * EDGE, width), f32), VMEM((taps, block + 2 * EDGE, chunk), bf16)],
    )(where, products, from_mate, from_outer, far, *bundles)

    order = (1, 3, 2)
    everyone = lax.all_to_all(spread, "seq", 0, 0, tiled=True)
    opposite = rotate(bundles[2], "mp", 2)
    bundles = [bundles[0], rotate(bundles[1], "mp", 1), rotate(bundles[3], "mp", 3), opposite]

    per_tile = 2 * channels * TILE
    thin = jax.ShapeDtypeStruct((most, 2, TILE), f32)
    slot = jax.ShapeDtypeStruct((2, frames), f32)
    reach = (2 * REACH + 1) * frames + 2 * TILE + 256
    near_shape = (NEAR, 2, 3, channels, TILE)
    far_shape = (most - NEAR, 2, 3, channels, TILE)
    ordered = [bundles[i] for i in (0, 1, 3, 2)]
    pred, offset, near, kept = call(
        functools.partial(forward_kernel, last_seq),
        "forward",
        flops=2 * per_tile * 2 * (taps * window + taps * channels),
        moved=2 * per_tile * 6,
        out_shape=(
            thin,
            jax.ShapeDtypeStruct((2,), jnp.int32),
            jax.ShapeDtypeStruct(near_shape, bf16),
            pltpu.HBM(far_shape, bf16),
        ),
        in_specs=[scalars()] + [whole()] * 8,
        out_specs=(whole(), scalars(), whole(), anywhere),
        scratch_shapes=[
            VMEM((2, window, TILE), f32),
            VMEM((2 * channels, taps * window), bf16),
            VMEM((2, channels, TILE), f32),
            VMEM(far_shape, bf16),
            pltpu.SemaphoreType.DMA((most - NEAR,)),
        ],
    )(where, to_mate, left, right, *ordered, turned)

    residual, kept, *slots = call(
        align_kernel,
        "align",
        vmem=4,
        moved=most * 8 * TILE * 8,
        out_shape=(thin, jax.ShapeDtypeStruct(far_shape, bf16)) + (slot,) * 5,
        in_specs=[scalars(), scalars()] + [whole()] * 7 + [anywhere],
        out_specs=(whole(),) * 7,
        scratch_shapes=[
            VMEM((8, reach), f32),
            VMEM((8, reach), f32),
            pltpu.SemaphoreType.DMA((most - NEAR,)),
        ],
    )(where, offset, everyone, pred, to_mate, left, right, far, bundles[1], in_hbm(kept))

    arrived = [
        lax.ppermute(slots[3], "seq", [(s, s ^ 1) for s in range(seq_size)]),
        lax.ppermute(slots[1], "seq", [(s, outer_of(s)) for s in range(seq_size)]),
        rotate(slots[4], "seq", REACH),
        rotate(slots[0], "seq", -REACH),
    ]

    sums = call(
        functools.partial(backward_kernel, last_seq),
        "backward",
        flops=2 * per_tile * 2 * (taps * share + taps * channels),
        moved=2 * per_tile * 6,
        out_shape=jax.ShapeDtypeStruct((taps * share, 2 * channels), bf16),
        in_specs=[scalars()] + [whole()] * 7,
        out_specs=whole(),
        scratch_shapes=[
            VMEM((2, share, TILE), f32),
            VMEM((taps * share, 2 * channels), f32),
            VMEM(conv_second.shape, bf16),
        ],
    )(where, to_mate, left, right, residual, near, kept, turned)

    merged = call(
        merge_kernel,
        "merge",
        vmem=4,
        moved=taps * share * channels * 8,
        out_shape=jax.ShapeDtypeStruct((taps * share + 16, frames // 2), bf16),
        in_specs=[whole()] * 6,
        out_specs=whole(),
    )(sums, slots[REACH], *arrived)

    mergeds = [merged, *(rotate(merged, "mp", d) for d in order)]
    predicted, row_grad = call(
        finish_kernel,
        "finish",
        vmem=8,
        flops=2 * block * features * taps * 2 * channels,
        moved=8 * taps * features * chunk,
        out_shape=(slot, jax.ShapeDtypeStruct((block, features), bf16)),
        in_specs=[scalars()] + [whole()] * 8,
        out_specs=(copied((2, frames)), copied((block, features))),
        scratch_shapes=[VMEM((taps, block, 2 * channels), bf16)],
    )(where, *(mergeds[i] for i in (0, 1, 3, 2)), *ordered)
    return (predicted, row_grad)


def solution(mesh):
    in_specs = (P("seq", None), P("seq"), P(None, None, "mp"), P(), P(), P(None, "seq"))
    out_specs = (P(None, "seq"), P("seq", "mp"))
    return jax.shard_map(body, mesh=mesh, in_specs=in_specs, out_specs=out_specs, check_vma=False)
```

```python
import functools

import jax
import jax.numpy as jnp
from jax import lax
from jax.experimental import pallas as pl
from jax.experimental.pallas import tpu as pltpu
from jax.sharding import PartitionSpec as P

EPSILON = 1e-05
TILE = 512
STRIDE = 508
LEAD = 3
HALO = 4
EDGE = 16
LONGEST = 40
REACH = 2
NEAR = 1
f32 = jnp.float32
bf16 = jnp.bfloat16
VMEM = pltpu.VMEM
SMEM = pltpu.SMEM


def whole():
    return pl.BlockSpec(memory_space=VMEM)


def copied(shape):
    return pl.BlockSpec(shape, lambda _: (0,) * len(shape))


def in_hbm(array):
    return pltpu.with_memory_space_constraint(array, pltpu.HBM)


def scalars():
    return pl.BlockSpec(memory_space=SMEM)


def call(kernel, name, *, flops=0, moved=0, vmem=24, **kwargs):
    return pl.pallas_call(
        kernel,
        name=name,
        grid=(1,),
        cost_estimate=pl.CostEstimate(flops=flops, bytes_accessed=moved, transcendentals=0),
        compiler_params=pltpu.CompilerParams(vmem_limit_bytes=vmem * 1024 * 1024),
        **kwargs,
    )


def rotate(block, axis, distance):
    size = lax.axis_size(axis)
    return lax.ppermute(block, axis, [(i, (i + distance) % size) for i in range(size)])


def pack_kernel(where_ref, dur_ref, targets_ref, readout_ref, head_ref, tail_ref, to_mate_ref, to_outer_ref):
    block = dur_ref.shape[1]
    frames = targets_ref.shape[1]
    channels = readout_ref.shape[1]
    even = jnp.bitwise_and(where_ref[0], 1) == 0
    tail = tail_ref[...].astype(f32)[16 - HALO : 16]
    head = head_ref[...].astype(f32)[0:HALO]
    rows = (jnp.where(even, tail, head), jnp.where(even, head, tail))
    readout = readout_ref[...].astype(f32)
    for out, halo in zip((to_mate_ref, to_outer_ref), rows):
        out[...] = jnp.zeros_like(out)
        out[0:2, 0:frames] = targets_ref[...]
        out[2:3, 0:block] = dur_ref[...].astype(f32)
        for q in range(2):
            out[3:4, q * channels : (q + 1) * channels] = readout[q : q + 1]
        out[HALO : 2 * HALO, :] = halo


def prepare_kernel(where_ref, dur_ref, rows_ref, conv_ref, second_ref, spread_ref, products_ref, *refs):
    bundle_refs, (turned_ref, wide_ref, sem) = refs[:4], refs[4:]
    wide_ref[...] = jnp.broadcast_to(dur_ref[...], wide_ref.shape)
    spread = pltpu.make_async_copy(wide_ref, spread_ref, sem)
    spread.start()
    taps, width, _ = conv_ref.shape
    block = rows_ref.shape[0]
    channels = second_ref.shape[2]
    members = len(bundle_refs)
    features = width // members
    low = taps * (block // members + 2 * EDGE)
    for k in range(taps):
        product = jnp.dot(rows_ref[...], conv_ref[k], preferred_element_type=f32)
        products_ref[k * block : (k + 1) * block, :] = product.astype(bf16)
    for d in range(members):
        target = lax.rem(where_ref[1] + d, members)
        at = pl.ds(pl.multiple_of(target * features, features), features)
        for k in range(taps):
            bundle_refs[d][low + k * features : low + (k + 1) * features, :] = conv_ref[k, at, :]
    for q in range(2):
        for k in range(taps):
            turned_ref[q, :, k * channels : (k + 1) * channels] = second_ref[q, k].T
    spread.wait()


def split(values):
    terms = []
    for _ in range(3):
        terms.append(values.astype(bf16).astype(f32))
        values = values - terms[-1]
    return terms


def pieces_kernel(where_ref, products_ref, mate_ref, outer_ref, far_ref, *refs):
    given_refs, bundle_refs, (left_ref, right_ref, halo_ref, table_ref) = refs[:4], refs[4:8], refs[8:]
    even = jnp.bitwise_and(where_ref[0], 1) == 0
    left_ref[...] = jnp.where(even, outer_ref[...], mate_ref[...])
    right_ref[...] = jnp.where(even, mate_ref[...], outer_ref[...])
    channels = products_ref.shape[1]
    members = len(bundle_refs)
    features = halo_ref.shape[1] // members
    taps = table_ref.shape[0]
    block = products_ref.shape[0] // taps
    share = block // members
    window = share + 2 * EDGE
    low = taps * window
    high = low + taps * features
    halo_ref[...] = jnp.zeros_like(halo_ref)
    halo_ref[EDGE - HALO : EDGE, :] = left_ref[HALO : 2 * HALO]
    halo_ref[EDGE : EDGE + HALO, :] = right_ref[HALO : 2 * HALO]
    for k in range(taps):
        product = jnp.zeros((2 * EDGE, channels), f32)
        for d in range(members):
            owner = lax.rem(where_ref[1] + d, members)
            part = halo_ref[:, pl.ds(pl.multiple_of(owner * features, features), features)].astype(bf16)
            cut = given_refs[d][low + k * features : low + (k + 1) * features, :]
            product = product + jnp.dot(part, cut, preferred_element_type=f32)
        table_ref[k, 0:EDGE, :] = product[0:EDGE].astype(bf16)
        table_ref[k, EDGE : EDGE + block, :] = products_ref[k * block : (k + 1) * block, :]
        table_ref[k, EDGE + block :, :] = product[EDGE:].astype(bf16)
    far = far_ref[...]
    parts = [
        term[:, c * channels : (c + 1) * channels]
        for term in split(far)
        for c in range(far.shape[1] // channels)
    ]
    parts = jnp.concatenate(parts, axis=0).astype(bf16)
    for d in range(members):
        target = lax.rem(where_ref[1] + d, members)
        at = pl.ds(pl.multiple_of(target * share, share), window)
        for k in range(taps):
            bundle_refs[d][k * window : (k + 1) * window, :] = table_ref[k, at, :]
        bundle_refs[d][high:, :] = parts


def share_bounds(where_ref, own_ref, left_ref, right_ref, last_seq, rows, first_row):
    block = 4 * (rows - 2 * (EDGE - first_row))
    share = block // 4
    s, m = where_ref[0], where_ref[1]
    lane = lax.broadcasted_iota(jnp.int32, (1, block), 1)
    near = jnp.where((lane >= block - HALO) & (s > 0), left_ref[2:3, 0:block], 0.0)
    far = jnp.where((lane < HALO) & (s < last_seq), right_ref[2:3, 0:block], 0.0)
    own = own_ref[2:3, 0:block]
    durations = jnp.concatenate([near, own, far], axis=1)
    phoneme = lax.broadcasted_iota(jnp.int32, (1, 3 * block), 1) - block
    begin = m * share
    row = lax.broadcasted_iota(jnp.int32, (rows, 3 * block), 0) + (begin + first_row - EDGE)
    at = jnp.broadcast_to(phoneme, (rows, 3 * block))
    spread = jnp.broadcast_to(durations, (rows, 3 * block))
    later = at >= begin

    def bound(limit):
        signed = jnp.where(later & (at < limit), spread, 0.0) - jnp.where(
            (at < begin) & (at >= limit), spread, 0.0
        )
        return jnp.sum(signed, axis=1, keepdims=True)

    count = jnp.sum(jnp.where((phoneme >= begin) & (phoneme < begin + share), durations, 0.0))
    skipped = jnp.sum(jnp.where((phoneme >= 0) & (phoneme < begin), durations, 0.0))
    return bound(row), bound(row + 1), count, skipped, jnp.sum(own)


def tiles_of(count):
    return lax.div(count.astype(jnp.int32) + (2 + STRIDE - 1), STRIDE)


def one_hot(frames, starts, ends):
    return jnp.where((frames >= starts) & (frames < ends), 1.0, 0.0).astype(bf16)


def local_frames(t):
    lane = lax.broadcasted_iota(jnp.int32, (1, TILE), 1)
    return (lane + (t * STRIDE - LEAD)).astype(f32), lane


def column_mean(values):
    return jnp.sum(values, axis=0, keepdims=True) * (1.0 / values.shape[0])


def with_neighbours(values):
    return jnp.concatenate(
        [
            pltpu.roll(values, 1, 1).astype(bf16),
            values.astype(bf16),
            pltpu.roll(values, TILE - 1, 1).astype(bf16),
        ],
        axis=0,
    )


def forward_kernel(
    last_seq,
    where_ref,
    own_ref,
    left_ref,
    right_ref,
    piece_ref,
    one_ref,
    two_ref,
    three_ref,
    kernel_ref,
    pred_ref,
    offset_ref,
    near_ref,
    far_kept_ref,
    bounds_ref,
    table_ref,
    weight_ref,
    more_ref,
    sems,
):
    channels = kernel_ref.shape[1]
    chunk = piece_ref.shape[1]
    taps = kernel_ref.shape[2] // channels
    window = bounds_ref.shape[1]
    depth = taps * window
    members = 2 * channels // chunk
    s, m = where_ref[0], where_ref[1]
    starts, ends, total, skipped, block_total = share_bounds(
        where_ref, own_ref, left_ref, right_ref, last_seq, window, 0
    )
    bounds_ref[0] = jnp.broadcast_to(starts, (window, TILE))
    bounds_ref[1] = jnp.broadcast_to(ends, (window, TILE))
    lowest = jnp.where(s == 0, -skipped, -1e9)
    end = jnp.where(s == last_seq, block_total - skipped, 1e9)
    for q in range(2):
        column = own_ref[:, q * channels : (q + 1) * channels].T
        weight_ref[q] = jnp.broadcast_to(column[:, 3:4], (channels, TILE))
    for d, source in enumerate((piece_ref, one_ref, two_ref, three_ref)):
        owner = lax.rem(m + members - d, members)
        table_ref[pl.ds(pl.multiple_of(owner * chunk, chunk), chunk), :] = source[0:depth, :].T

    for q in range(2):
        column = own_ref[:, q * channels : (q + 1) * channels].T
        weight_ref[q] = jnp.broadcast_to(column[:, 3:4], (channels, TILE))
    offset_ref[0] = skipped.astype(jnp.int32)
    offset_ref[1] = total.astype(jnp.int32)
    pred_ref[...] = jnp.zeros_like(pred_ref)

    def work(t, kept_ref, at):
        frames, lane = local_frames(t)
        selector = jnp.concatenate(
            [one_hot(frames + (k - 1.0), bounds_ref[0], bounds_ref[1]) for k in range(taps)], axis=0
        )
        inside = jnp.where((frames >= lowest) & (frames < end), 1.0, 0.0)
        answered = jnp.where((lane >= 2) & (lane < 2 + STRIDE), inside, 0.0)
        both = range(2)
        first = [
            jnp.dot(table_ref[q * channels : (q + 1) * channels, :], selector, preferred_element_type=f32)
            for q in both
        ]
        act = [
            (jnp.maximum(x, 0.0) + jnp.log(1.0 + jnp.exp(-jnp.abs(x)))).astype(bf16).astype(f32) for x in first
        ]
        centered = [x - column_mean(x) for x in act]
        inverse_one = [lax.rsqrt(column_mean(x * x) + EPSILON) for x in centered]
        stacked = [with_neighbours(centered[q] * (inverse_one[q] * inside)) for q in both]
        second = [jnp.dot(kernel_ref[q], stacked[q], preferred_element_type=f32) for q in both]
        for q in both:
            kept_ref[at, q, 2] = ((1.0 - jnp.exp(-act[q])) * (inverse_one[q] * answered)).astype(bf16)
            kept_ref[at, q, 0] = stacked[q][channels : 2 * channels]
        soft = [jnp.maximum(x, 0.0) + jnp.log(1.0 + jnp.exp(-jnp.abs(x))) for x in second]
        sigmoid = [jnp.exp(second[q] - soft[q]) for q in both]
        centered = [x - column_mean(x) for x in soft]
        inverse_two = [lax.rsqrt(column_mean(x * x) + EPSILON) for x in centered]
        normed = [centered[q] * inverse_two[q] for q in both]
        weighted_mean = [column_mean(normed[q] * weight_ref[q]) for q in both]
        for q in both:
            weights = weight_ref[q]
            pred_ref[t, q : q + 1, :] = weighted_mean[q] * float(channels)
            factor = (weights - column_mean(weights) - normed[q] * weighted_mean[q]) * sigmoid[q]
            kept_ref[at, q, 1] = (factor * (inverse_two[q] * inside)).astype(bf16)

    def step(t, carry):
        work(t, near_ref, t)
        return carry

    def far_step(t, carry):
        work(t, more_ref, t - NEAR)
        pltpu.make_async_copy(more_ref.at[t - NEAR], far_kept_ref.at[t - NEAR], sems.at[t - NEAR]).start()
        return carry

    def wait(t, carry):
        pltpu.make_async_copy(more_ref.at[t - NEAR], far_kept_ref.at[t - NEAR], sems.at[t - NEAR]).wait()
        return carry

    tiles = tiles_of(total)
    lax.fori_loop(0, jnp.minimum(tiles, NEAR), step, 0)
    lax.fori_loop(NEAR, tiles, far_step, 0)
    lax.fori_loop(NEAR, tiles, wait, 0)


def align_kernel(
    where_ref,
    offset_ref,
    spread_ref,
    pred_ref,
    own_ref,
    left_ref,
    right_ref,
    far_ref,
    one_ref,
    far_kept_ref,
    residual_ref,
    kept_ref,
    *refs,
):
    slot_refs, (window_ref, placed_ref, sems) = refs[:5], refs[5:]
    s, m = where_ref[0], where_ref[1]
    chunk = one_ref.shape[1]
    frames_each = far_ref.shape[1]
    count = offset_ref[1]
    tiles = lax.div(count + (2 + STRIDE - 1), STRIDE)

    def fetch(t, carry):
        pltpu.make_async_copy(far_kept_ref.at[t - NEAR], kept_ref.at[t - NEAR], sems.at[t - NEAR]).start()
        return carry

    def wait(t, carry):
        pltpu.make_async_copy(far_kept_ref.at[t - NEAR], kept_ref.at[t - NEAR], sems.at[t - NEAR]).wait()
        return carry

    lax.fori_loop(NEAR, tiles, fetch, 0)
    seq = lax.broadcasted_iota(jnp.int32, spread_ref.shape, 0)
    before = jnp.sum(jnp.where(seq < s, spread_ref[...].astype(f32), 0.0))
    offset = before.astype(jnp.int32) + offset_ref[0] - (s - REACH) * frames_each
    window_ref[...] = jnp.zeros_like(window_ref)
    placed_ref[...] = jnp.zeros_like(placed_ref)
    parts = one_ref[one_ref.shape[0] - 3 * 2 * frames_each // chunk :, :].astype(f32)
    terms = [parts[i * 2 * frames_each // chunk : (i + 1) * 2 * frames_each // chunk] for i in range(3)]
    terms = terms[0] + terms[1] + terms[2]
    other = jnp.concatenate([terms[2 * c : 2 * c + 2] for c in range(frames_each // chunk)], axis=1)
    even = jnp.bitwise_and(m, 1) == 0
    here = far_ref[...]
    beside = (jnp.where(even, here, other), left_ref[0:2], own_ref[0:2], right_ref[0:2], jnp.where(even, other, here))
    for i, source in enumerate(beside):
        window_ref[0:2, TILE + i * frames_each : TILE + (i + 1) * frames_each] = source
    exact_lane = lax.broadcasted_iota(jnp.int32, (2, TILE), 1)
    exact = (exact_lane >= LEAD) & (exact_lane < LEAD + STRIDE)

    def step(t, carry):
        at = jnp.clip(TILE + offset + t * STRIDE - LEAD, 0, window_ref.shape[1] - TILE - 128)
        rest = jnp.bitwise_and(at, 127)
        near = pl.ds(pl.multiple_of(at - rest, 128), TILE + 128)
        taken = pltpu.roll(window_ref[:, near], TILE + 128 - rest, 1)[0:2, 0:TILE]
        values = pred_ref[t]
        residual_ref[t] = values - taken
        own = exact & (exact_lane + (t * STRIDE - LEAD) < count)
        moved = jnp.concatenate([jnp.where(own, values, 0.0), jnp.zeros((2, 128), f32)], axis=1)
        moved = jnp.concatenate([moved, jnp.zeros((6, TILE + 128), f32)], axis=0)
        placed_ref[:, near] = placed_ref[:, near] + pltpu.roll(moved, rest, 1)
        return carry

    lax.fori_loop(0, tiles, step, 0)
    even = jnp.bitwise_and(s, 1) == 0
    slots = [placed_ref[0:2, TILE + i * frames_each : TILE + (i + 1) * frames_each] for i in range(5)]
    slots[1], slots[3] = jnp.where(even, slots[1], slots[3]), jnp.where(even, slots[3], slots[1])
    for slot, values in zip(slot_refs, slots):
        slot[...] = values
    lax.fori_loop(NEAR, tiles, wait, 0)


def backward_kernel(
    last_seq,
    where_ref,
    own_ref,
    left_ref,
    right_ref,
    residual_ref,
    near_ref,
    more_ref,
    turned_ref,
    out_ref,
    bounds_ref,
    sums_ref,
    conv_ref,
):
    taps = conv_ref.shape[1]
    channels = conv_ref.shape[2]
    share = bounds_ref.shape[1]
    starts, ends, count, _, _ = share_bounds(where_ref, own_ref, left_ref, right_ref, last_seq, share, EDGE)
    bounds_ref[0] = jnp.broadcast_to(starts, (share, TILE))
    bounds_ref[1] = jnp.broadcast_to(ends, (share, TILE))
    sums_ref[...] = jnp.zeros_like(sums_ref)
    for q in range(2):
        for k in range(taps):
            conv_ref[q, k] = turned_ref[q, :, k * channels : (k + 1) * channels].T

    def work(t, kept_ref, at):
        frames, _ = local_frames(t)
        selector = jnp.concatenate(
            [one_hot(frames + (k - 1.0), bounds_ref[0], bounds_ref[1]) for k in range(taps)], axis=0
        )
        both = range(2)
        stacked = [with_neighbours(kept_ref[at, q, 1].astype(f32) * residual_ref[t, q : q + 1, :]) for q in both]
        grad_hidden = [jnp.zeros((channels, TILE), f32) for q in both]
        for k in range(taps):
            for q in both:
                part = stacked[q][(taps - 1 - k) * channels : (taps - k) * channels]
                grad_hidden[q] = grad_hidden[q] + jnp.dot(conv_ref[q, k], part, preferred_element_type=f32)
        normed = [kept_ref[at, q, 0].astype(f32) for q in both]
        first_mean = [column_mean(x) for x in grad_hidden]
        second_mean = [column_mean(grad_hidden[q] * normed[q]) for q in both]
        grad_first = [
            (grad_hidden[q] - first_mean[q] - normed[q] * second_mean[q]) * kept_ref[at, q, 2].astype(f32)
            for q in both
        ]
        for q in both:
            sums_ref[:, q * channels : (q + 1) * channels] += lax.dot_general(
                selector, grad_first[q].astype(bf16), (((1,), (1,)), ((), ())), preferred_element_type=f32
            )

    def step(t, carry):
        work(t, near_ref, t)
        return carry

    def far_step(t, carry):
        work(t, more_ref, t - NEAR)
        return carry

    tiles = tiles_of(count)
    lax.fori_loop(0, jnp.minimum(tiles, NEAR), step, 0)
    lax.fori_loop(NEAR, tiles, far_step, 0)
    out_ref[...] = sums_ref[...].astype(bf16)


def merge_kernel(sums_ref, own_ref, *refs):
    arrived, out_ref = refs[:-1], refs[-1]
    depth = sums_ref.shape[0]
    half = out_ref.shape[1]
    out_ref[0:depth, :] = sums_ref[...]
    left = own_ref[...]
    for source in arrived:
        left = left + source[...]
    parts = [term[:, i * half : (i + 1) * half] for term in split(left) for i in range(2)]
    parts.append(jnp.zeros((4, half), f32))
    out_ref[depth:, :] = jnp.concatenate(parts, axis=0).astype(bf16)


def finish_kernel(where_ref, *refs):
    merged_refs, bundle_refs, (pred_ref, out_ref, rows_ref) = refs[:4], refs[4:8], refs[8:]
    taps = rows_ref.shape[0]
    chunk = bundle_refs[0].shape[1]
    features = out_ref.shape[1]
    members = len(merged_refs)
    low = taps * (rows_ref.shape[1] // members + 2 * EDGE)
    share = rows_ref.shape[1] // members
    depth = taps * share
    half = merged_refs[0].shape[1]
    pred = jnp.zeros((2, 2 * half), f32)
    for d, source in enumerate(merged_refs):
        owner = lax.rem(where_ref[1] + members - d, members)
        at = pl.ds(pl.multiple_of(owner * share, share), share)
        for k in range(taps):
            rows_ref[k, at, :] = source[k * share : (k + 1) * share, :]
        parts = source[depth:, :].astype(f32)
        for i in range(3):
            pred = pred + jnp.concatenate([parts[4 * i : 4 * i + 2], parts[4 * i + 2 : 4 * i + 4]], axis=1)
    pred_ref[...] = pred
    total = jnp.zeros(out_ref.shape, f32)
    for pair in (0, 2):
        owners = [lax.rem(where_ref[1] + members - d, members) for d in (pair, pair + 1)]
        sources = bundle_refs[pair : pair + 2]
        for k in range(taps):
            rows = [rows_ref[k, :, pl.ds(pl.multiple_of(owner * chunk, chunk), chunk)] for owner in owners]
            cuts = [source[low + k * features : low + (k + 1) * features, :] for source in sources]
            total = total + lax.dot_general(
                jnp.concatenate(rows, axis=1),
                jnp.concatenate(cuts, axis=1),
                (((1,), (1,)), ((), ())),
                preferred_element_type=f32,
            )
    out_ref[...] = total.astype(bf16)


def body(phoneme_rows, durations, conv_first, conv_second, readout, targets):
    seq_size = lax.axis_size("seq")
    members = lax.axis_size("mp")
    block, width = phoneme_rows.shape
    frames = targets.shape[1]
    taps, _, chunk = conv_first.shape
    channels = conv_second.shape[2]
    features = width // members
    share = block // members
    window = share + 2 * EDGE
    most = -(-(share * LONGEST + 2) // STRIDE)
    last_seq = seq_size - 1
    where = jnp.stack([lax.axis_index("seq"), lax.axis_index("mp")]).astype(jnp.int32)
    anywhere = pl.BlockSpec(memory_space=pl.ANY)
    pack = jax.ShapeDtypeStruct((2 * HALO, width), f32)
    dur = durations.reshape(1, block)

    to_mate, to_outer = call(
        pack_kernel,
        "pack",
        vmem=4,
        moved=2 * 32 * width,
        out_shape=(pack, pack),
        in_specs=[
            scalars(),
            copied((1, block)),
            copied(targets.shape),
            copied(readout.shape),
            pl.BlockSpec((16, width), lambda _: (0, 0)),
            pl.BlockSpec((16, width), lambda _: (block // 16 - 1, 0)),
        ],
        out_specs=(whole(),) * 2,
    )(where, in_hbm(dur), in_hbm(targets), in_hbm(readout), in_hbm(phoneme_rows), in_hbm(phoneme_rows))

    def outer_of(s):
        return (s + (1 if s % 2 else -1)) % seq_size

    from_mate = lax.ppermute(to_mate, "seq", [(s, s ^ 1) for s in range(seq_size)])
    from_outer = lax.ppermute(to_outer, "seq", [(s, outer_of(s)) for s in range(seq_size)])
    far = lax.ppermute(
        targets,
        ("seq", "mp"),
        [
            ((s + (-REACH if m % 2 == 0 else REACH)) % seq_size * members + m, s * members + m)
            for s in range(seq_size)
            for m in range(members)
        ],
    )

    bundle = jax.ShapeDtypeStruct((taps * (window + features) + 3 * 2 * frames // chunk, chunk), bf16)
    spread, products, *made = call(
        prepare_kernel,
        "prepare",
        vmem=12,
        flops=2 * block * width * taps * chunk,
        moved=2 * block * width + 2 * taps * width * chunk + 4 * taps * channels * channels,
        out_shape=(pltpu.HBM((seq_size, block), jnp.int32), jax.ShapeDtypeStruct((taps * block, chunk), bf16))
        + (bundle,) * 4
        + (jax.ShapeDtypeStruct((2, channels, taps * channels), bf16),),
        in_specs=[
            scalars(),
            copied((1, block)),
            copied(phoneme_rows.shape),
            copied(conv_first.shape),
            copied(conv_second.shape),
        ],
        out_specs=(anywhere,) + (whole(),) * 6,
        scratch_shapes=[VMEM((seq_size, block), jnp.int32), pltpu.SemaphoreType.DMA],
    )(where, in_hbm(dur), in_hbm(phoneme_rows), in_hbm(conv_first), in_hbm(conv_second))
    bundles, turned = made[:4], made[4]

    *bundles, left, right = call(
        pieces_kernel,
        "pieces",
        vmem=8,
        flops=2 * 2 * EDGE * width * taps * chunk,
        moved=2 * taps * width * chunk,
        out_shape=(bundle,) * 4 + (pack,) * 2,
        in_specs=[scalars()] + [whole()] * 8,
        out_specs=(whole(),) * 6,
        input_output_aliases={5 + d: d for d in range(4)},
        scratch_shapes=[VMEM((2 * EDGE, width), f32), VMEM((taps, block + 2 * EDGE, chunk), bf16)],
    )(where, products, from_mate, from_outer, far, *bundles)

    order = (1, 3, 2)
    everyone = lax.all_to_all(spread, "seq", 0, 0, tiled=True)
    opposite = rotate(bundles[2], "mp", 2)
    bundles = [bundles[0], rotate(bundles[1], "mp", 1), rotate(bundles[3], "mp", 3), opposite]

    per_tile = 2 * channels * TILE
    thin = jax.ShapeDtypeStruct((most, 2, TILE), f32)
    slot = jax.ShapeDtypeStruct((2, frames), f32)
    reach = (2 * REACH + 1) * frames + 2 * TILE + 256
    near_shape = (NEAR, 2, 3, channels, TILE)
    far_shape = (most - NEAR, 2, 3, channels, TILE)
    ordered = [bundles[i] for i in (0, 1, 3, 2)]
    pred, offset, near, kept = call(
        functools.partial(forward_kernel, last_seq),
        "forward",
        flops=2 * per_tile * 2 * (taps * window + taps * channels),
        moved=2 * per_tile * 6,
        out_shape=(
            thin,
            jax.ShapeDtypeStruct((2,), jnp.int32),
            jax.ShapeDtypeStruct(near_shape, bf16),
            pltpu.HBM(far_shape, bf16),
        ),
        in_specs=[scalars()] + [whole()] * 8,
        out_specs=(whole(), scalars(), whole(), anywhere),
        scratch_shapes=[
            VMEM((2, window, TILE), f32),
            VMEM((2 * channels, taps * window), bf16),
            VMEM((2, channels, TILE), f32),
            VMEM(far_shape, bf16),
            pltpu.SemaphoreType.DMA((most - NEAR,)),
        ],
    )(where, to_mate, left, right, *ordered, turned)

    residual, kept, *slots = call(
        align_kernel,
        "align",
        vmem=4,
        moved=most * 8 * TILE * 8,
        out_shape=(thin, jax.ShapeDtypeStruct(far_shape, bf16)) + (slot,) * 5,
        in_specs=[scalars(), scalars()] + [whole()] * 7 + [anywhere],
        out_specs=(whole(),) * 7,
        scratch_shapes=[
            VMEM((8, reach), f32),
            VMEM((8, reach), f32),
            pltpu.SemaphoreType.DMA((most - NEAR,)),
        ],
    )(where, offset, everyone, pred, to_mate, left, right, far, bundles[1], in_hbm(kept))

    arrived = [
        lax.ppermute(slots[3], "seq", [(s, s ^ 1) for s in range(seq_size)]),
        lax.ppermute(slots[1], "seq", [(s, outer_of(s)) for s in range(seq_size)]),
        rotate(slots[4], "seq", REACH),
        rotate(slots[0], "seq", -REACH),
    ]

    sums = call(
        functools.partial(backward_kernel, last_seq),
        "backward",
        flops=2 * per_tile * 2 * (taps * share + taps * channels),
        moved=2 * per_tile * 6,
        out_shape=jax.ShapeDtypeStruct((taps * share, 2 * channels), bf16),
        in_specs=[scalars()] + [whole()] * 7,
        out_specs=whole(),
        scratch_shapes=[
            VMEM((2, share, TILE), f32),
            VMEM((taps * share, 2 * channels), f32),
            VMEM(conv_second.shape, bf16),
        ],
    )(where, to_mate, left, right, residual, near, kept, turned)

    merged = call(
        merge_kernel,
        "merge",
        vmem=4,
        moved=taps * share * channels * 8,
        out_shape=jax.ShapeDtypeStruct((taps * share + 16, frames // 2), bf16),
        in_specs=[whole()] * 6,
        out_specs=whole(),
    )(sums, slots[REACH], *arrived)

    mergeds = [merged, *(rotate(merged, "mp", d) for d in order)]
    predicted, row_grad = call(
        finish_kernel,
        "finish",
        vmem=8,
        flops=2 * block * features * taps * 2 * channels,
        moved=8 * taps * features * chunk,
        out_shape=(slot, jax.ShapeDtypeStruct((block, features), bf16)),
        in_specs=[scalars()] + [whole()] * 8,
        out_specs=(copied((2, frames)), copied((block, features))),
        scratch_shapes=[VMEM((taps, block, 2 * channels), bf16)],
    )(where, *(mergeds[i] for i in (0, 1, 3, 2)), *ordered)
    return (predicted, row_grad)


def solution(mesh):
    in_specs = (P("seq", None), P("seq"), P(None, None, "mp"), P(), P(), P(None, "seq"))
    out_specs = (P(None, "seq"), P("seq", "mp"))
    return jax.shard_map(body, mesh=mesh, in_specs=in_specs, out_specs=out_specs, check_vma=False)
```

```python
import functools

import jax
import jax.numpy as jnp
from jax import lax
from jax.experimental import pallas as pl
from jax.experimental.pallas import tpu as pltpu
from jax.sharding import PartitionSpec as P

EPSILON = 1e-05
TILE = 512
STRIDE = 508
LEAD = 3
HALO = 4
EDGE = 16
LONGEST = 40
REACH = 2
NEAR = 1
f32 = jnp.float32
bf16 = jnp.bfloat16
VMEM = pltpu.VMEM
SMEM = pltpu.SMEM


def whole():
    return pl.BlockSpec(memory_space=VMEM)


def copied(shape):
    return pl.BlockSpec(shape, lambda _: (0,) * len(shape))


def in_hbm(array):
    return pltpu.with_memory_space_constraint(array, pltpu.HBM)


def scalars():
    return pl.BlockSpec(memory_space=SMEM)


def call(kernel, name, *, flops=0, moved=0, vmem=24, **kwargs):
    return pl.pallas_call(
        kernel,
        name=name,
        grid=(1,),
        cost_estimate=pl.CostEstimate(flops=flops, bytes_accessed=moved, transcendentals=0),
        compiler_params=pltpu.CompilerParams(vmem_limit_bytes=vmem * 1024 * 1024),
        **kwargs,
    )


def rotate(block, axis, distance):
    size = lax.axis_size(axis)
    return lax.ppermute(block, axis, [(i, (i + distance) % size) for i in range(size)])


def pack_kernel(where_ref, dur_ref, targets_ref, readout_ref, head_ref, tail_ref, to_mate_ref, to_outer_ref):
    block = dur_ref.shape[1]
    frames = targets_ref.shape[1]
    channels = readout_ref.shape[1]
    even = jnp.bitwise_and(where_ref[0], 1) == 0
    tail = tail_ref[...].astype(f32)[16 - HALO : 16]
    head = head_ref[...].astype(f32)[0:HALO]
    rows = (jnp.where(even, tail, head), jnp.where(even, head, tail))
    readout = readout_ref[...].astype(f32)
    for out, halo in zip((to_mate_ref, to_outer_ref), rows):
        out[...] = jnp.zeros_like(out)
        out[0:2, 0:frames] = targets_ref[...]
        out[2:3, 0:block] = dur_ref[...].astype(f32)
        for q in range(2):
            out[3:4, q * channels : (q + 1) * channels] = readout[q : q + 1]
        out[HALO : 2 * HALO, :] = halo


def prepare_kernel(where_ref, dur_ref, rows_ref, conv_ref, second_ref, spread_ref, products_ref, *refs):
    bundle_refs, (turned_ref, wide_ref, sem) = refs[:4], refs[4:]
    wide_ref[...] = jnp.broadcast_to(dur_ref[...], wide_ref.shape)
    spread = pltpu.make_async_copy(wide_ref, spread_ref, sem)
    spread.start()
    taps, width, _ = conv_ref.shape
    block = rows_ref.shape[0]
    channels = second_ref.shape[2]
    members = len(bundle_refs)
    features = width // members
    low = taps * (block // members + 2 * EDGE)
    for k in range(taps):
        product = jnp.dot(rows_ref[...], conv_ref[k], preferred_element_type=f32)
        products_ref[k * block : (k + 1) * block, :] = product.astype(bf16)
    for d in range(members):
        target = lax.rem(where_ref[1] + d, members)
        at = pl.ds(pl.multiple_of(target * features, features), features)
        for k in range(taps):
            bundle_refs[d][low + k * features : low + (k + 1) * features, :] = conv_ref[k, at, :]
    for q in range(2):
        for k in range(taps):
            turned_ref[q, :, k * channels : (k + 1) * channels] = second_ref[q, k].T
    spread.wait()


def split(values):
    terms = []
    for _ in range(3):
        terms.append(values.astype(bf16).astype(f32))
        values = values - terms[-1]
    return terms


def pieces_kernel(where_ref, products_ref, mate_ref, outer_ref, far_ref, *refs):
    given_refs, bundle_refs, (left_ref, right_ref, halo_ref, table_ref) = refs[:4], refs[4:8], refs[8:]
    even = jnp.bitwise_and(where_ref[0], 1) == 0
    left_ref[...] = jnp.where(even, outer_ref[...], mate_ref[...])
    right_ref[...] = jnp.where(even, mate_ref[...], outer_ref[...])
    channels = products_ref.shape[1]
    members = len(bundle_refs)
    features = halo_ref.shape[1] // members
    taps = table_ref.shape[0]
    block = products_ref.shape[0] // taps
    share = block // members
    window = share + 2 * EDGE
    low = taps * window
    high = low + taps * features
    halo_ref[...] = jnp.zeros_like(halo_ref)
    halo_ref[EDGE - HALO : EDGE, :] = left_ref[HALO : 2 * HALO]
    halo_ref[EDGE : EDGE + HALO, :] = right_ref[HALO : 2 * HALO]
    for k in range(taps):
        product = jnp.zeros((2 * EDGE, channels), f32)
        for d in range(members):
            owner = lax.rem(where_ref[1] + d, members)
            part = halo_ref[:, pl.ds(pl.multiple_of(owner * features, features), features)].astype(bf16)
            cut = given_refs[d][low + k * features : low + (k + 1) * features, :]
            product = product + jnp.dot(part, cut, preferred_element_type=f32)
        table_ref[k, 0:EDGE, :] = product[0:EDGE].astype(bf16)
        table_ref[k, EDGE : EDGE + block, :] = products_ref[k * block : (k + 1) * block, :]
        table_ref[k, EDGE + block :, :] = product[EDGE:].astype(bf16)
    far = far_ref[...]
    parts = [
        term[:, c * channels : (c + 1) * channels]
        for term in split(far)
        for c in range(far.shape[1] // channels)
    ]
    parts = jnp.concatenate(parts, axis=0).astype(bf16)
    for d in range(members):
        target = lax.rem(where_ref[1] + d, members)
        at = pl.ds(pl.multiple_of(target * share, share), window)
        for k in range(taps):
            bundle_refs[d][k * window : (k + 1) * window, :] = table_ref[k, at, :]
        bundle_refs[d][high:, :] = parts


def share_bounds(where_ref, own_ref, left_ref, right_ref, last_seq, rows, first_row):
    block = 4 * (rows - 2 * (EDGE - first_row))
    share = block // 4
    s, m = where_ref[0], where_ref[1]
    lane = lax.broadcasted_iota(jnp.int32, (1, block), 1)
    near = jnp.where((lane >= block - HALO) & (s > 0), left_ref[2:3, 0:block], 0.0)
    far = jnp.where((lane < HALO) & (s < last_seq), right_ref[2:3, 0:block], 0.0)
    own = own_ref[2:3, 0:block]
    durations = jnp.concatenate([near, own, far], axis=1)
    phoneme = lax.broadcasted_iota(jnp.int32, (1, 3 * block), 1) - block
    begin = m * share
    row = lax.broadcasted_iota(jnp.int32, (rows, 3 * block), 0) + (begin + first_row - EDGE)
    at = jnp.broadcast_to(phoneme, (rows, 3 * block))
    spread = jnp.broadcast_to(durations, (rows, 3 * block))
    later = at >= begin

    def bound(limit):
        signed = jnp.where(later & (at < limit), spread, 0.0) - jnp.where(
            (at < begin) & (at >= limit), spread, 0.0
        )
        return jnp.sum(signed, axis=1, keepdims=True)

    count = jnp.sum(jnp.where((phoneme >= begin) & (phoneme < begin + share), durations, 0.0))
    skipped = jnp.sum(jnp.where((phoneme >= 0) & (phoneme < begin), durations, 0.0))
    return bound(row), bound(row + 1), count, skipped, jnp.sum(own)


def tiles_of(count):
    return lax.div(count.astype(jnp.int32) + (2 + STRIDE - 1), STRIDE)


def one_hot(frames, starts, ends):
    return jnp.where((frames >= starts) & (frames < ends), 1.0, 0.0).astype(bf16)


def local_frames(t):
    lane = lax.broadcasted_iota(jnp.int32, (1, TILE), 1)
    return (lane + (t * STRIDE - LEAD)).astype(f32), lane


def column_mean(values):
    return jnp.sum(values, axis=0, keepdims=True) * (1.0 / values.shape[0])


def with_neighbours(values):
    return jnp.concatenate(
        [
            pltpu.roll(values, 1, 1).astype(bf16),
            values.astype(bf16),
            pltpu.roll(values, TILE - 1, 1).astype(bf16),
        ],
        axis=0,
    )


def forward_kernel(
    last_seq,
    where_ref,
    own_ref,
    left_ref,
    right_ref,
    piece_ref,
    one_ref,
    two_ref,
    three_ref,
    kernel_ref,
    pred_ref,
    offset_ref,
    near_ref,
    far_kept_ref,
    bounds_ref,
    table_ref,
    weight_ref,
    more_ref,
    sems,
):
    channels = kernel_ref.shape[1]
    chunk = piece_ref.shape[1]
    taps = kernel_ref.shape[2] // channels
    window = bounds_ref.shape[1]
    depth = taps * window
    members = 2 * channels // chunk
    s, m = where_ref[0], where_ref[1]
    starts, ends, total, skipped, block_total = share_bounds(
        where_ref, own_ref, left_ref, right_ref, last_seq, window, 0
    )
    bounds_ref[0] = jnp.broadcast_to(starts, (window, TILE))
    bounds_ref[1] = jnp.broadcast_to(ends, (window, TILE))
    lowest = jnp.where(s == 0, -skipped, -1e9)
    end = jnp.where(s == last_seq, block_total - skipped, 1e9)
    for q in range(2):
        column = own_ref[:, q * channels : (q + 1) * channels].T
        weight_ref[q] = jnp.broadcast_to(column[:, 3:4], (channels, TILE))
    for d, source in enumerate((piece_ref, one_ref, two_ref, three_ref)):
        owner = lax.rem(m + members - d, members)
        table_ref[pl.ds(pl.multiple_of(owner * chunk, chunk), chunk), :] = source[0:depth, :].T

    for q in range(2):
        column = own_ref[:, q * channels : (q + 1) * channels].T
        weight_ref[q] = jnp.broadcast_to(column[:, 3:4], (channels, TILE))
    offset_ref[0] = skipped.astype(jnp.int32)
    offset_ref[1] = total.astype(jnp.int32)
    pred_ref[...] = jnp.zeros_like(pred_ref)

    def work(t, kept_ref, at):
        frames, lane = local_frames(t)
        selector = jnp.concatenate(
            [one_hot(frames + (k - 1.0), bounds_ref[0], bounds_ref[1]) for k in range(taps)], axis=0
        )
        inside = jnp.where((frames >= lowest) & (frames < end), 1.0, 0.0)
        answered = jnp.where((lane >= 2) & (lane < 2 + STRIDE), inside, 0.0)
        both = range(2)
        first = [
            jnp.dot(table_ref[q * channels : (q + 1) * channels, :], selector, preferred_element_type=f32)
            for q in both
        ]
        act = [
            (jnp.maximum(x, 0.0) + jnp.log(1.0 + jnp.exp(-jnp.abs(x)))).astype(bf16).astype(f32) for x in first
        ]
        centered = [x - column_mean(x) for x in act]
        inverse_one = [lax.rsqrt(column_mean(x * x) + EPSILON) for x in centered]
        stacked = [with_neighbours(centered[q] * (inverse_one[q] * inside)) for q in both]
        second = [jnp.dot(kernel_ref[q], stacked[q], preferred_element_type=f32) for q in both]
        for q in both:
            kept_ref[at, q, 2] = ((1.0 - jnp.exp(-act[q])) * (inverse_one[q] * answered)).astype(bf16)
            kept_ref[at, q, 0] = stacked[q][channels : 2 * channels]
        soft = [jnp.maximum(x, 0.0) + jnp.log(1.0 + jnp.exp(-jnp.abs(x))) for x in second]
        sigmoid = [jnp.exp(second[q] - soft[q]) for q in both]
        centered = [x - column_mean(x) for x in soft]
        inverse_two = [lax.rsqrt(column_mean(x * x) + EPSILON) for x in centered]
        normed = [centered[q] * inverse_two[q] for q in both]
        weighted_mean = [column_mean(normed[q] * weight_ref[q]) for q in both]
        for q in both:
            weights = weight_ref[q]
            pred_ref[t, q : q + 1, :] = weighted_mean[q] * float(channels)
            factor = (weights - column_mean(weights) - normed[q] * weighted_mean[q]) * sigmoid[q]
            kept_ref[at, q, 1] = (factor * (inverse_two[q] * inside)).astype(bf16)

    def step(t, carry):
        work(t, near_ref, t)
        return carry

    def far_step(t, carry):
        work(t, more_ref, t - NEAR)
        pltpu.make_async_copy(more_ref.at[t - NEAR], far_kept_ref.at[t - NEAR], sems.at[t - NEAR]).start()
        return carry

    def wait(t, carry):
        pltpu.make_async_copy(more_ref.at[t - NEAR], far_kept_ref.at[t - NEAR], sems.at[t - NEAR]).wait()
        return carry

    tiles = tiles_of(total)
    lax.fori_loop(0, jnp.minimum(tiles, NEAR), step, 0)
    lax.fori_loop(NEAR, tiles, far_step, 0)
    lax.fori_loop(NEAR, tiles, wait, 0)


def align_kernel(
    where_ref,
    offset_ref,
    spread_ref,
    pred_ref,
    own_ref,
    left_ref,
    right_ref,
    far_ref,
    one_ref,
    far_kept_ref,
    residual_ref,
    kept_ref,
    *refs,
):
    slot_refs, (window_ref, placed_ref, sems) = refs[:5], refs[5:]
    s, m = where_ref[0], where_ref[1]
    chunk = one_ref.shape[1]
    frames_each = far_ref.shape[1]
    count = offset_ref[1]
    tiles = lax.div(count + (2 + STRIDE - 1), STRIDE)

    def fetch(t, carry):
        pltpu.make_async_copy(far_kept_ref.at[t - NEAR], kept_ref.at[t - NEAR], sems.at[t - NEAR]).start()
        return carry

    def wait(t, carry):
        pltpu.make_async_copy(far_kept_ref.at[t - NEAR], kept_ref.at[t - NEAR], sems.at[t - NEAR]).wait()
        return carry

    lax.fori_loop(NEAR, tiles, fetch, 0)
    seq = lax.broadcasted_iota(jnp.int32, spread_ref.shape, 0)
    before = jnp.sum(jnp.where(seq < s, spread_ref[...].astype(f32), 0.0))
    offset = before.astype(jnp.int32) + offset_ref[0] - (s - REACH) * frames_each
    window_ref[...] = jnp.zeros_like(window_ref)
    placed_ref[...] = jnp.zeros_like(placed_ref)
    parts = one_ref[one_ref.shape[0] - 3 * 2 * frames_each // chunk :, :].astype(f32)
    terms = [parts[i * 2 * frames_each // chunk : (i + 1) * 2 * frames_each // chunk] for i in range(3)]
    terms = terms[0] + terms[1] + terms[2]
    other = jnp.concatenate([terms[2 * c : 2 * c + 2] for c in range(frames_each // chunk)], axis=1)
    even = jnp.bitwise_and(m, 1) == 0
    here = far_ref[...]
    beside = (jnp.where(even, here, other), left_ref[0:2], own_ref[0:2], right_ref[0:2], jnp.where(even, other, here))
    for i, source in enumerate(beside):
        window_ref[0:2, TILE + i * frames_each : TILE + (i + 1) * frames_each] = source
    exact_lane = lax.broadcasted_iota(jnp.int32, (2, TILE), 1)
    exact = (exact_lane >= LEAD) & (exact_lane < LEAD + STRIDE)

    def step(t, carry):
        at = jnp.clip(TILE + offset + t * STRIDE - LEAD, 0, window_ref.shape[1] - TILE - 128)
        rest = jnp.bitwise_and(at, 127)
        near = pl.ds(pl.multiple_of(at - rest, 128), TILE + 128)
        taken = pltpu.roll(window_ref[:, near], TILE + 128 - rest, 1)[0:2, 0:TILE]
        values = pred_ref[t]
        residual_ref[t] = values - taken
        own = exact & (exact_lane + (t * STRIDE - LEAD) < count)
        moved = jnp.concatenate([jnp.where(own, values, 0.0), jnp.zeros((2, 128), f32)], axis=1)
        moved = jnp.concatenate([moved, jnp.zeros((6, TILE + 128), f32)], axis=0)
        placed_ref[:, near] = placed_ref[:, near] + pltpu.roll(moved, rest, 1)
        return carry

    lax.fori_loop(0, tiles, step, 0)
    even = jnp.bitwise_and(s, 1) == 0
    slots = [placed_ref[0:2, TILE + i * frames_each : TILE + (i + 1) * frames_each] for i in range(5)]
    slots[1], slots[3] = jnp.where(even, slots[1], slots[3]), jnp.where(even, slots[3], slots[1])
    for slot, values in zip(slot_refs, slots):
        slot[...] = values
    lax.fori_loop(NEAR, tiles, wait, 0)


def backward_kernel(
    last_seq,
    where_ref,
    own_ref,
    left_ref,
    right_ref,
    residual_ref,
    near_ref,
    more_ref,
    turned_ref,
    out_ref,
    bounds_ref,
    sums_ref,
    conv_ref,
):
    channels = conv_ref.shape[1]
    taps = conv_ref.shape[2] // channels
    share = bounds_ref.shape[1]
    starts, ends, count, _, _ = share_bounds(where_ref, own_ref, left_ref, right_ref, last_seq, share, EDGE)
    bounds_ref[0] = jnp.broadcast_to(starts, (share, TILE))
    bounds_ref[1] = jnp.broadcast_to(ends, (share, TILE))
    sums_ref[...] = jnp.zeros_like(sums_ref)
    for q in range(2):
        for k in range(taps):
            at = (taps - 1 - k) * channels
            conv_ref[q, :, at : at + channels] = turned_ref[q, :, k * channels : (k + 1) * channels].T

    def work(t, kept_ref, at):
        frames, _ = local_frames(t)
        selector = jnp.concatenate(
            [one_hot(frames + (k - 1.0), bounds_ref[0], bounds_ref[1]) for k in range(taps)], axis=0
        )
        both = range(2)
        stacked = [with_neighbours(kept_ref[at, q, 1].astype(f32) * residual_ref[t, q : q + 1, :]) for q in both]
        grad_hidden = [jnp.dot(conv_ref[q], stacked[q], preferred_element_type=f32) for q in both]
        normed = [kept_ref[at, q, 0].astype(f32) for q in both]
        first_mean = [column_mean(x) for x in grad_hidden]
        second_mean = [column_mean(grad_hidden[q] * normed[q]) for q in both]
        grad_first = [
            (grad_hidden[q] - first_mean[q] - normed[q] * second_mean[q]) * kept_ref[at, q, 2].astype(f32)
            for q in both
        ]
        for q in both:
            sums_ref[:, q * channels : (q + 1) * channels] += lax.dot_general(
                selector, grad_first[q].astype(bf16), (((1,), (1,)), ((), ())), preferred_element_type=f32
            )

    def step(t, carry):
        work(t, near_ref, t)
        return carry

    def far_step(t, carry):
        work(t, more_ref, t - NEAR)
        return carry

    tiles = tiles_of(count)
    lax.fori_loop(0, jnp.minimum(tiles, NEAR), step, 0)
    lax.fori_loop(NEAR, tiles, far_step, 0)
    out_ref[...] = sums_ref[...].astype(bf16)


def merge_kernel(sums_ref, own_ref, *refs):
    arrived, out_ref = refs[:-1], refs[-1]
    depth = sums_ref.shape[0]
    half = out_ref.shape[1]
    out_ref[0:depth, :] = sums_ref[...]
    left = own_ref[...]
    for source in arrived:
        left = left + source[...]
    parts = [term[:, i * half : (i + 1) * half] for term in split(left) for i in range(2)]
    parts.append(jnp.zeros((4, half), f32))
    out_ref[depth:, :] = jnp.concatenate(parts, axis=0).astype(bf16)


def finish_kernel(where_ref, *refs):
    merged_refs, bundle_refs, (pred_ref, out_ref, rows_ref) = refs[:4], refs[4:8], refs[8:]
    taps = rows_ref.shape[0]
    chunk = bundle_refs[0].shape[1]
    features = out_ref.shape[1]
    members = len(merged_refs)
    low = taps * (rows_ref.shape[1] // members + 2 * EDGE)
    share = rows_ref.shape[1] // members
    depth = taps * share
    half = merged_refs[0].shape[1]
    pred = jnp.zeros((2, 2 * half), f32)
    for d, source in enumerate(merged_refs):
        owner = lax.rem(where_ref[1] + members - d, members)
        at = pl.ds(pl.multiple_of(owner * share, share), share)
        for k in range(taps):
            rows_ref[k, at, :] = source[k * share : (k + 1) * share, :]
        parts = source[depth:, :].astype(f32)
        for i in range(3):
            pred = pred + jnp.concatenate([parts[4 * i : 4 * i + 2], parts[4 * i + 2 : 4 * i + 4]], axis=1)
    pred_ref[...] = pred
    total = jnp.zeros(out_ref.shape, f32)
    for pair in (0, 2):
        owners = [lax.rem(where_ref[1] + members - d, members) for d in (pair, pair + 1)]
        sources = bundle_refs[pair : pair + 2]
        for k in range(taps):
            rows = [rows_ref[k, :, pl.ds(pl.multiple_of(owner * chunk, chunk), chunk)] for owner in owners]
            cuts = [source[low + k * features : low + (k + 1) * features, :] for source in sources]
            total = total + lax.dot_general(
                jnp.concatenate(rows, axis=1),
                jnp.concatenate(cuts, axis=1),
                (((1,), (1,)), ((), ())),
                preferred_element_type=f32,
            )
    out_ref[...] = total.astype(bf16)


def body(phoneme_rows, durations, conv_first, conv_second, readout, targets):
    seq_size = lax.axis_size("seq")
    members = lax.axis_size("mp")
    block, width = phoneme_rows.shape
    frames = targets.shape[1]
    taps, _, chunk = conv_first.shape
    channels = conv_second.shape[2]
    features = width // members
    share = block // members
    window = share + 2 * EDGE
    most = -(-(share * LONGEST + 2) // STRIDE)
    last_seq = seq_size - 1
    where = jnp.stack([lax.axis_index("seq"), lax.axis_index("mp")]).astype(jnp.int32)
    anywhere = pl.BlockSpec(memory_space=pl.ANY)
    pack = jax.ShapeDtypeStruct((2 * HALO, width), f32)
    dur = durations.reshape(1, block)

    to_mate, to_outer = call(
        pack_kernel,
        "pack",
        vmem=4,
        moved=2 * 32 * width,
        out_shape=(pack, pack),
        in_specs=[
            scalars(),
            copied((1, block)),
            copied(targets.shape),
            copied(readout.shape),
            pl.BlockSpec((16, width), lambda _: (0, 0)),
            pl.BlockSpec((16, width), lambda _: (block // 16 - 1, 0)),
        ],
        out_specs=(whole(),) * 2,
    )(where, in_hbm(dur), in_hbm(targets), in_hbm(readout), in_hbm(phoneme_rows), in_hbm(phoneme_rows))

    def outer_of(s):
        return (s + (1 if s % 2 else -1)) % seq_size

    from_mate = lax.ppermute(to_mate, "seq", [(s, s ^ 1) for s in range(seq_size)])
    from_outer = lax.ppermute(to_outer, "seq", [(s, outer_of(s)) for s in range(seq_size)])
    far = lax.ppermute(
        targets,
        ("seq", "mp"),
        [
            ((s + (-REACH if m % 2 == 0 else REACH)) % seq_size * members + m, s * members + m)
            for s in range(seq_size)
            for m in range(members)
        ],
    )

    bundle = jax.ShapeDtypeStruct((taps * (window + features) + 3 * 2 * frames // chunk, chunk), bf16)
    spread, products, *made = call(
        prepare_kernel,
        "prepare",
        vmem=12,
        flops=2 * block * width * taps * chunk,
        moved=2 * block * width + 2 * taps * width * chunk + 4 * taps * channels * channels,
        out_shape=(pltpu.HBM((seq_size, block), jnp.int32), jax.ShapeDtypeStruct((taps * block, chunk), bf16))
        + (bundle,) * 4
        + (jax.ShapeDtypeStruct((2, channels, taps * channels), bf16),),
        in_specs=[
            scalars(),
            copied((1, block)),
            copied(phoneme_rows.shape),
            copied(conv_first.shape),
            copied(conv_second.shape),
        ],
        out_specs=(anywhere,) + (whole(),) * 6,
        scratch_shapes=[VMEM((seq_size, block), jnp.int32), pltpu.SemaphoreType.DMA],
    )(where, in_hbm(dur), in_hbm(phoneme_rows), in_hbm(conv_first), in_hbm(conv_second))
    bundles, turned = made[:4], made[4]

    *bundles, left, right = call(
        pieces_kernel,
        "pieces",
        vmem=8,
        flops=2 * 2 * EDGE * width * taps * chunk,
        moved=2 * taps * width * chunk,
        out_shape=(bundle,) * 4 + (pack,) * 2,
        in_specs=[scalars()] + [whole()] * 8,
        out_specs=(whole(),) * 6,
        input_output_aliases={5 + d: d for d in range(4)},
        scratch_shapes=[VMEM((2 * EDGE, width), f32), VMEM((taps, block + 2 * EDGE, chunk), bf16)],
    )(where, products, from_mate, from_outer, far, *bundles)

    order = (1, 3, 2)
    everyone = lax.all_to_all(spread, "seq", 0, 0, tiled=True)
    opposite = rotate(bundles[2], "mp", 2)
    bundles = [bundles[0], rotate(bundles[1], "mp", 1), rotate(bundles[3], "mp", 3), opposite]

    per_tile = 2 * channels * TILE
    thin = jax.ShapeDtypeStruct((most, 2, TILE), f32)
    slot = jax.ShapeDtypeStruct((2, frames), f32)
    reach = (2 * REACH + 1) * frames + 2 * TILE + 256
    near_shape = (NEAR, 2, 3, channels, TILE)
    far_shape = (most - NEAR, 2, 3, channels, TILE)
    ordered = [bundles[i] for i in (0, 1, 3, 2)]
    pred, offset, near, kept = call(
        functools.partial(forward_kernel, last_seq),
        "forward",
        flops=2 * per_tile * 2 * (taps * window + taps * channels),
        moved=2 * per_tile * 6,
        out_shape=(
            thin,
            jax.ShapeDtypeStruct((2,), jnp.int32),
            jax.ShapeDtypeStruct(near_shape, bf16),
            pltpu.HBM(far_shape, bf16),
        ),
        in_specs=[scalars()] + [whole()] * 8,
        out_specs=(whole(), scalars(), whole(), anywhere),
        scratch_shapes=[
            VMEM((2, window, TILE), f32),
            VMEM((2 * channels, taps * window), bf16),
            VMEM((2, channels, TILE), f32),
            VMEM(far_shape, bf16),
            pltpu.SemaphoreType.DMA((most - NEAR,)),
        ],
    )(where, to_mate, left, right, *ordered, turned)

    residual, kept, *slots = call(
        align_kernel,
        "align",
        vmem=4,
        moved=most * 8 * TILE * 8,
        out_shape=(thin, jax.ShapeDtypeStruct(far_shape, bf16)) + (slot,) * 5,
        in_specs=[scalars(), scalars()] + [whole()] * 7 + [anywhere],
        out_specs=(whole(),) * 7,
        scratch_shapes=[
            VMEM((8, reach), f32),
            VMEM((8, reach), f32),
            pltpu.SemaphoreType.DMA((most - NEAR,)),
        ],
    )(where, offset, everyone, pred, to_mate, left, right, far, bundles[1], in_hbm(kept))

    arrived = [
        lax.ppermute(slots[3], "seq", [(s, s ^ 1) for s in range(seq_size)]),
        lax.ppermute(slots[1], "seq", [(s, outer_of(s)) for s in range(seq_size)]),
        rotate(slots[4], "seq", REACH),
        rotate(slots[0], "seq", -REACH),
    ]

    sums = call(
        functools.partial(backward_kernel, last_seq),
        "backward",
        flops=2 * per_tile * 2 * (taps * share + taps * channels),
        moved=2 * per_tile * 6,
        out_shape=jax.ShapeDtypeStruct((taps * share, 2 * channels), bf16),
        in_specs=[scalars()] + [whole()] * 7,
        out_specs=whole(),
        scratch_shapes=[
            VMEM((2, share, TILE), f32),
            VMEM((taps * share, 2 * channels), f32),
            VMEM(turned.shape, bf16),
        ],
    )(where, to_mate, left, right, residual, near, kept, turned)

    merged = call(
        merge_kernel,
        "merge",
        vmem=4,
        moved=taps * share * channels * 8,
        out_shape=jax.ShapeDtypeStruct((taps * share + 16, frames // 2), bf16),
        in_specs=[whole()] * 6,
        out_specs=whole(),
    )(sums, slots[REACH], *arrived)

    mergeds = [merged, *(rotate(merged, "mp", d) for d in order)]
    predicted, row_grad = call(
        finish_kernel,
        "finish",
        vmem=8,
        flops=2 * block * features * taps * 2 * channels,
        moved=8 * taps * features * chunk,
        out_shape=(slot, jax.ShapeDtypeStruct((block, features), bf16)),
        in_specs=[scalars()] + [whole()] * 8,
        out_specs=(copied((2, frames)), copied((block, features))),
        scratch_shapes=[VMEM((taps, block, 2 * channels), bf16)],
    )(where, *(mergeds[i] for i in (0, 1, 3, 2)), *ordered)
    return (predicted, row_grad)


def solution(mesh):
    in_specs = (P("seq", None), P("seq"), P(None, None, "mp"), P(), P(), P(None, "seq"))
    out_specs = (P(None, "seq"), P("seq", "mp"))
    return jax.shard_map(body, mesh=mesh, in_specs=in_specs, out_specs=out_specs, check_vma=False)
```
